256 devices in a mesh: dp: 16 (over z, y_hi), expert: 16 (over y_lo, x, core).
Axes of the slice: x: 4, y: 4 (y_hi: 2, y_lo: 2; y = y_hi * 2 + y_lo), z: 8, core: 2. Of those that a mesh axis runs over, the one named last changes fastest.
Arguments:
- tokens: bfloat16 [2048, 7168], P('dp', 'expert'), may hold values from -6 to 6
- cotangent: bfloat16 [2048, 7168], P('dp', 'expert'), may hold values from -6 to 6
- gates: bfloat16 [2048, 2], P('dp'), may hold values from 0.19921875 to 2.5
- expert_ids: int32 [2048, 2], P('dp'), may hold values from 0 to 16, as said below
- w_gate: bfloat16 [16, 7168, 2048], P('dp', None, 'expert'), may hold values from -0.0625 to 0.0625
- w_up: bfloat16 [16, 7168, 2048], P('dp', None, 'expert'), may hold values from -0.0625 to 0.0625
- w_down: bfloat16 [16, 2048, 7168], P('dp', 'expert'), may hold values from -0.125 to 0.125
Outputs:
- grad_tokens: bfloat16 [2048, 7168], P('dp', 'expert')
- gate_grads: float32 [2048, 2], P('dp')
- grad_gate: bfloat16 [16, 7168, 2048], P('dp', None, 'expert')
- grad_up: bfloat16 [16, 7168, 2048], P('dp', None, 'expert')
- grad_down: bfloat16 [16, 2048, 7168], P('dp', 'expert')
The draws below stay inside these ranges and needn't reach their ends.
Inputs may be any that keep to these rules, and one draw needn't show every extreme that they name: `expert_ids`: column 0 names one of the experts 0 to half of 16 minus 1 and column 1 one of the others, or the value 16 for a choice outside this window. The 128 tokens of one index of dp route at most 8 tokens to one expert; in each column one expert, the same for every index of dp, receives exactly 8 tokens from every index of dp.
All inputs are finite; a program needn't handle non-finite values.
Results may differ from the reference program's by a relative error of at most 0.024.
Values may be sent and summed in bfloat16 or wider, within the bound.
A program may use at most 128 MiB of HBM per device.

```python
import jax
import jax.numpy as jnp
from jax import lax

D = 7168
H = 2048
TOK_DEV = 128
ROUTES = 2
HID_DEV = 128
CAP = 8
EXPERTS = 16
TOKENS = 2048
N_DP = 16


def draw_expert_ids(key, part):
    key = jax.random.fold_in(key, 11)
    half = EXPERTS // 2
    blocks = TOKENS // TOK_DEV
    hot_key, count_key, perm_key = jax.random.split(key, 3)
    hot = jax.random.randint(hot_key, (2,), 0, half)
    counts = jax.random.randint(count_key, (blocks, 2, half), 0, 2 * CAP // 3 + 1)
    local = jnp.arange(half, dtype=jnp.int32)
    counts = jnp.where(local[None, None, :] == hot[None, :, None], CAP, counts)
    ends = jnp.cumsum(counts, axis=2)
    perm_keys = jax.random.split(perm_key, blocks * 2)
    orders = jax.vmap(lambda single: jax.random.permutation(single, TOK_DEV))(perm_keys)
    ranks = jnp.argsort(orders, axis=1, stable=True).reshape(blocks, 2, TOK_DEV)
    label = jnp.sum((ranks[:, :, :, None] >= ends[:, :, None, :]).astype(jnp.int32), axis=3)
    column = jnp.arange(2, dtype=jnp.int32)[None, :, None]
    ids = jnp.where(label < half, label + column * half, EXPERTS)
    return jnp.transpose(ids, (0, 2, 1)).reshape(TOKENS, 2).astype(jnp.int32)


def block_scale(stream_key, shape, cuts, low, largest):
    loudness = 1.0
    for position, shards_of in cuts:
        steps = jax.random.uniform(jax.random.fold_in(jax.random.fold_in(stream_key, 6), position), (shards_of,), jnp.float32, low / len(cuts), largest / len(cuts))
        loudness = loudness * jnp.repeat(jnp.exp(steps), shape[position] // shards_of).reshape((-1,) + (1,) * (len(shape) - 1 - position))
    return loudness


def gaussian(key, extent, spread, limit, shards=(), kind=jnp.bfloat16):
    entries = spread * jax.random.normal(key, extent, jnp.float32)
    if shards:
        entries = entries * block_scale(key, extent, shards, -0.22, 0.18)
    return jnp.clip(entries, -limit, limit).astype(kind)


def setup_inputs(seed: int = 0) -> dict:
    arg_keys = jax.random.split(jax.random.key(seed), 8)
    tokens = gaussian(arg_keys[0], (TOKENS, D), 1.0, 6.0, ((0, 16), (1, 16)))
    cotangent = gaussian(arg_keys[1], (TOKENS, D), 1.0, 6.0, ((0, 16), (1, 16)))
    gates = jnp.clip(0.19921875 + 2.3007812 * jax.random.uniform(arg_keys[2], (TOKENS, ROUTES), jnp.float32) ** block_scale(arg_keys[2], (TOKENS, ROUTES), ((0, 16),), -0.2, 0.2), 0.19921875, 2.5).astype(jnp.bfloat16)
    expert_ids = draw_expert_ids(jax.random.fold_in(arg_keys[7], 71), 0)
    w_gate = gaussian(arg_keys[4], (EXPERTS, D, H), D ** -0.5, 0.0625, ((0, 16), (2, 16)))
    w_up = gaussian(arg_keys[5], (EXPERTS, D, H), D ** -0.5, 0.0625, ((0, 16), (2, 16)))
    w_down = gaussian(arg_keys[6], (EXPERTS, H, D), H ** -0.5, 0.125, ((0, 16), (1, 16)))
    return dict(tokens=tokens, cotangent=cotangent, gates=gates, expert_ids=expert_ids, w_gate=w_gate, w_up=w_up, w_down=w_down)


def slot_grads(x_rows, d_rows, g_rows, gate_m, up_m, down_m):
    pre_gate = jnp.dot(x_rows, gate_m, preferred_element_type=jnp.float32)
    pre_up = jnp.dot(x_rows, up_m, preferred_element_type=jnp.float32)
    sig = jax.nn.sigmoid(pre_gate)
    act = pre_gate * sig
    hidden = (act * pre_up).astype(jnp.bfloat16)
    back = lax.dot_general(d_rows, down_m, (((1,), (1,)), ((), ())), preferred_element_type=jnp.float32)
    gate_terms = jnp.sum(back * hidden.astype(jnp.float32), axis=1)
    dhid = g_rows[:, None] * back
    scaled = (g_rows[:, None] * d_rows.astype(jnp.float32)).astype(jnp.bfloat16)
    grad_down = lax.dot_general(hidden, scaled, (((0,), (0,)), ((), ())), preferred_element_type=jnp.float32).astype(jnp.bfloat16)
    d_gate = (dhid * pre_up * sig * (1.0 + pre_gate * (1.0 - sig))).astype(jnp.bfloat16)
    d_up = (dhid * act).astype(jnp.bfloat16)
    grad_gate = lax.dot_general(x_rows, d_gate, (((0,), (0,)), ((), ())), preferred_element_type=jnp.float32).astype(jnp.bfloat16)
    grad_up = lax.dot_general(x_rows, d_up, (((0,), (0,)), ((), ())), preferred_element_type=jnp.float32).astype(jnp.bfloat16)
    blocks = H // HID_DEV
    rows = x_rows.shape[0]
    dg_blocks = d_gate.astype(jnp.float32).reshape(rows, blocks, HID_DEV)
    du_blocks = d_up.astype(jnp.float32).reshape(rows, blocks, HID_DEV)
    gm_blocks = gate_m.astype(jnp.float32).reshape(gate_m.shape[0], blocks, HID_DEV)
    um_blocks = up_m.astype(jnp.float32).reshape(up_m.shape[0], blocks, HID_DEV)
    partial_rows = jnp.einsum("sbh,dbh->bsd", dg_blocks, gm_blocks) + jnp.einsum("sbh,dbh->bsd", du_blocks, um_blocks)
    row_grads = jnp.sum(partial_rows.astype(jnp.bfloat16).astype(jnp.float32), axis=0)
    return grad_gate, grad_up, grad_down, row_grads, gate_terms


def reference(tokens, cotangent, gates, expert_ids, w_gate, w_up, w_down):
    most = N_DP * CAP
    gate_f = gates.astype(jnp.float32)

    def one(carry, inputs):
        grad_x, gate_acc = carry
        label, gate_m, up_m, down_m = inputs
        hit = expert_ids == label
        member = jnp.any(hit, axis=1)
        route = jnp.sum(jnp.where(hit, gate_f, jnp.float32(0.0)), axis=1)
        where = jnp.nonzero(member, size=most, fill_value=0)[0].astype(jnp.int32)
        valid = jnp.arange(most, dtype=jnp.int32) < jnp.sum(member.astype(jnp.int32))
        x_rows = jnp.where(valid[:, None], tokens[where], jnp.zeros((), tokens.dtype))
        d_rows = jnp.where(valid[:, None], cotangent[where], jnp.zeros((), cotangent.dtype))
        g_rows = jnp.where(valid, route[where], jnp.float32(0.0))
        grad_gate, grad_up, grad_down, row_grads, gate_terms = slot_grads(x_rows, d_rows, g_rows, gate_m, up_m, down_m)
        grad_x = grad_x.at[where].add(jnp.where(valid[:, None], row_grads, jnp.float32(0.0)))
        gate_vec = jnp.zeros((tokens.shape[0],), jnp.float32).at[where].add(jnp.where(valid, gate_terms, jnp.float32(0.0)))
        gate_acc = gate_acc + jnp.where(hit, gate_vec[:, None], jnp.float32(0.0))
        return (grad_x, gate_acc), (grad_gate, grad_up, grad_down)

    start = (jnp.zeros(tokens.shape, jnp.float32), jnp.zeros(expert_ids.shape, jnp.float32))
    labels = jnp.arange(EXPERTS, dtype=jnp.int32)
    (grad_x, gate_acc), (grad_gate, grad_up, grad_down) = lax.scan(one, start, (labels, w_gate, w_up, w_down))
    return grad_x.astype(jnp.bfloat16), gate_acc, grad_gate, grad_up, grad_down
```

```python
import functools

import jax
import jax.numpy as jnp
from jax import lax
from jax.experimental import pallas as pl
from jax.experimental.pallas import tpu as pltpu
from jax.sharding import PartitionSpec as P

MESH = pl.DeviceIdType.MESH
BF = jnp.bfloat16
F32 = jnp.float32

CAP = 8
NDP = 16
NEX = 16
F = 448
FA = 256
FB = F - FA
HB = FB // 2
HA = FA // 2
C = 2 * F
D = NEX * F
HID = 128
TOK = 128
SLOTS = NDP * CAP
RB = F + 16


def iota(shape, dim):
    return lax.broadcasted_iota(jnp.int32, shape, dim)


def split_gate(row):
    hi = row.astype(BF).astype(F32)
    lo = row - hi
    r = iota((16, row.shape[1]), 0)
    return jnp.where(r == 0, hi, jnp.where(r == 1, lo, 0.0)).astype(BF)


def comm_kernel(
    tok_ref, cot_ref, ids_ref, gates_ref, wg_hbm, wu_hbm, wd_hbm,
    ret_out, pick_out, all_out, dd_out, hg_out,
    wgu, wd, ext, sa, sb, ra, rb, al, pre, back, dd, hg, tsend, tsib, rsend, rrecv, rpad, retb, ret,
    w_sem, out_sem, da_send, da_recv, db_send, db_recv, g_send, g_recv, sib_send, sib_recv,
    ts_send, ts_recv, r_send, r_recv, b_send, b_recv,
):
    me = lax.axis_index("dp")
    j = lax.axis_index("expert")
    y, x, c = j // 8, (j // 2) % 4, j % 2

    def dev(yy, xx, cc):
        return yy * 8 + xx * 2 + cc

    xr, xl, xo = (x + 1) % 4, (x + 3) % 4, (x + 2) % 4
    yo = 1 - y
    sib, xp, xm, yp = dev(y, x, 1 - c), dev(y, xr, c), dev(y, xl, c), dev(yo, x, c)

    barrier = pltpu.get_barrier_semaphore()
    for i in range(1, NDP):
        pl.semaphore_signal(barrier, inc=1, device_id=((me + i) % NDP, j), device_id_type=MESH)
    others = [(sib,)]
    chips = [(yy, xx) for yy in (y, yo) for xx in (x, xr, xl, xo)][1:]
    for yy, xx in chips:
        pl.semaphore_signal(barrier, inc=1, device_id=(me, dev(yy, xx, c)), device_id_type=MESH)
    pl.semaphore_signal(barrier, inc=1, device_id=(me, sib), device_id_type=MESH)

    loads = [
        pltpu.make_async_copy(wg_hbm.at[0], wgu.at[:, 0:HID], w_sem.at[0]),
        pltpu.make_async_copy(wu_hbm.at[0], wgu.at[:, HID : 2 * HID], w_sem.at[1]),
        pltpu.make_async_copy(wd_hbm.at[0], wd, w_sem.at[2]),
    ]
    for load in loads:
        load.start()

    col = iota((TOK, 256), 1)
    ids = ids_ref[...]
    chosen = jnp.where(col < 128, ids[:, 0:1], ids[:, 1:2])
    member = chosen == col // 16
    tri = (iota((TOK, TOK), 1) < iota((TOK, TOK), 0)).astype(F32).astype(BF)
    before = jnp.dot(tri, member.astype(F32).astype(BF), preferred_element_type=F32)
    pick = jnp.where(
        jnp.logical_and(member, before == (col % 8).astype(F32)), 1.0, 0.0
    )
    is_x = (col % 16) < 8
    pick_out[...] = pick.astype(BF)
    pick2 = jnp.concatenate(
        [jnp.where(is_x, pick, 0.0), jnp.where(is_x, 0.0, pick)], axis=0
    ).astype(BF)
    ext[:, 384:512] = jnp.zeros((2 * TOK, 128), BF)
    ext[0:TOK, 0:F] = tok_ref[...]
    ext[TOK : 2 * TOK, 0:F] = cot_ref[...]
    gates = gates_ref[...].astype(F32)
    lane = iota((TOK, 128), 1)
    ext[0:TOK, 384:512] = jnp.where(
        lane == 64,
        gates[:, 0:1],
        jnp.where(lane == 65, gates[:, 1:2], ext[0:TOK, 384:512].astype(F32)),
    ).astype(BF)
    slots = lax.dot_general(
        pick2, ext[...], (((0,), (0,)), ((), ())), preferred_element_type=F32
    ).astype(BF)
    sa[...] = slots[:, 0:256].reshape(NDP, 16, 256)
    sb[...] = slots[:, 256:512].reshape(NDP, 16, 256)

    pl.semaphore_wait(barrier, NDP - 1 + len(chips) + 1)

    def dispatch(src, dst, send, recv):
        copies = []
        for i in range(1, NDP):
            to = (me + i) % NDP
            copy = pltpu.make_async_remote_copy(
                src_ref=src.at[to], dst_ref=dst.at[me],
                send_sem=send.at[i], recv_sem=recv.at[i],
                device_id=(to, j), device_id_type=MESH,
            )
            copy.start()
            copies.append(copy)
        dst[pl.ds(me, 1)] = src[pl.ds(me, 1)]
        return copies

    copies_a = dispatch(sa, ra, da_send, da_recv)
    copies_b = dispatch(sb, rb, db_send, db_recv)

    r = iota((256, 256), 0)
    k = iota((256, 256), 1)
    kk = k % 128
    perm = jnp.where(r == (kk // 8) * 16 + (k // 128) * 8 + kk % 8, 1.0, 0.0).astype(BF)

    def turned(buf):
        return lax.dot_general(
            buf[...].reshape(256, 256), perm, (((0,), (0,)), ((), ())),
            preferred_element_type=F32,
        )

    def rows(b, lo, n):
        return al.at[pl.ds(pl.multiple_of(b * F + lo, 16), n)]

    sends = []

    def push(b, lo, n, to, s):
        copy = pltpu.make_async_remote_copy(
            src_ref=rows(b, lo, n), dst_ref=rows(b, lo, n),
            send_sem=g_send.at[s], recv_sem=g_recv.at[s],
            device_id=(me, to), device_id_type=MESH,
        )
        copy.start()
        sends.append(copy)

    def share(b, lo, n, s):
        copy = pltpu.make_async_remote_copy(
            src_ref=rows(b, lo, n), dst_ref=rows(b, lo, n),
            send_sem=sib_send.at[s], recv_sem=sib_recv.at[s],
            device_id=(me, sib), device_id_type=MESH,
        )
        copy.start()
        sends.append(copy)

    def got(b, lo, n, s):
        pltpu.make_async_remote_copy(
            src_ref=rows(b, lo, n), dst_ref=rows(b, lo, n),
            send_sem=g_send.at[s], recv_sem=g_recv.at[s],
            device_id=(me, sib), device_id_type=MESH,
        ).wait_recv()

    def shared(b, lo, n, s):
        pltpu.make_async_remote_copy(
            src_ref=rows(b, lo, n), dst_ref=rows(b, lo, n),
            send_sem=sib_send.at[s], recv_sem=sib_recv.at[s],
            device_id=(me, sib), device_id_type=MESH,
        ).wait_recv()

    b_own, b_xr, b_xl, b_xo = (dev(y, xx, c) for xx in (x, xr, xl, xo))
    o_own, o_xr, o_xl, o_xo = (dev(yo, xx, c) for xx in (x, xr, xl, xo))

    for copy in copies_a:
        copy.wait_recv()
    al[pl.ds(pl.multiple_of(j * F, 16), FA), :] = turned(ra).astype(BF)
    push(b_own, 0, FA, yp, 0)
    push(b_own, 0, FA, xp, 1)
    push(b_own, 0, FA, xm, 2)
    share(b_own, 0, FA, 0)

    for copy in copies_b:
        copy.wait_recv()
    second = turned(rb)
    al[pl.ds(pl.multiple_of(j * F + FA, 16), FB), :] = second[0:FB].astype(BF)
    gate_row = jnp.where(me < NDP // 2, second[FB : FB + 1, 0:128], second[FB + 1 : FB + 2, 0:128])
    push(b_own, FA, FB, yp, 3)
    push(b_own, FA, FB, xp, 4)
    push(b_own, FA, FB, xm, 5)
    share(b_own, FA, FB, 1)

    pre[...] = jnp.zeros_like(pre)
    back[...] = jnp.zeros_like(back)
    for load in loads:
        load.wait()

    def forward(chip):
        at = pl.ds(pl.multiple_of(chip * C, 128), C)
        block = al[at, :]
        pre[...] += lax.dot_general(
            block[:, 0:128], wgu[at, :], (((0,), (0,)), ((), ())), preferred_element_type=F32
        )
        back[...] += jnp.dot(wd[:, at], block[:, 128:256], preferred_element_type=F32)

    got(o_own, 0, FA, 0)
    push(o_own, 0, FA, xp, 6)
    push(o_own, 0, FA, xm, 7)
    share(o_own, 0, FA, 2)
    got(b_xl, FA, FB, 4)
    push(b_xl, FA, HB, xp, 8)
    push(b_xl, FA, FB, yp, 9)
    share(b_xl, FA, FB, 3)
    got(b_xr, FA, FB, 5)
    push(b_xr, FA + HB, HB, xm, 10)
    push(b_xr, FA, FB, yp, 11)
    share(b_xr, FA, FB, 4)
    got(b_xl, 0, FA, 1)
    push(b_xl, 0, HA, xp, 12)
    share(b_xl, 0, FA, 5)
    got(b_xr, 0, FA, 2)
    push(b_xr, HA, HA, xm, 13)
    share(b_xr, 0, FA, 6)

    sib_own = dev(y, x, 1 - c)
    shared(sib_own, 0, FA, 0)
    shared(sib_own, FA, FB, 1)
    forward(y * 4 + x)

    got(b_xo, FA, HB, 8)
    push(b_xo, FA, HB, yp, 14)
    share(b_xo, FA, HB, 7)
    got(b_xo, FA + HB, HB, 10)
    push(b_xo, FA + HB, HB, yp, 15)
    share(b_xo, FA + HB, HB, 8)
    got(o_xl, 0, FA, 6)
    push(o_xl, 0, HA, xp, 16)
    share(o_xl, 0, FA, 9)
    got(o_xr, 0, FA, 7)
    push(o_xr, HA, HA, xm, 17)
    share(o_xr, 0, FA, 10)
    got(o_own, FA, FB, 3)
    share(o_own, FA, FB, 11)

    n_xr, n_xl, n_xo = (dev(y, xx, 1 - c) for xx in (xr, xl, xo))
    m_own, m_xr, m_xl, m_xo = (dev(yo, xx, 1 - c) for xx in (x, xr, xl, xo))
    shared(n_xl, FA, FB, 3)
    shared(n_xl, 0, FA, 5)
    forward(y * 4 + xl)
    got(o_xl, FA, FB, 9)
    share(o_xl, FA, FB, 12)
    shared(n_xr, FA, FB, 4)
    shared(n_xr, 0, FA, 6)
    forward(y * 4 + xr)
    got(o_xr, FA, FB, 11)
    share(o_xr, FA, FB, 13)
    shared(m_own, 0, FA, 2)
    shared(m_own, FA, FB, 11)
    forward(yo * 4 + x)
    got(b_xo, 0, HA, 12)
    share(b_xo, 0, HA, 14)
    got(b_xo, HA, HA, 13)
    share(b_xo, HA, HA, 15)
    shared(m_xl, 0, FA, 9)
    shared(m_xl, FA, FB, 12)
    forward(yo * 4 + xl)
    shared(m_xr, 0, FA, 10)
    shared(m_xr, FA, FB, 13)
    forward(yo * 4 + xr)
    got(o_xo, 0, HA, 16)
    share(o_xo, 0, HA, 16)
    got(o_xo, HA, HA, 17)
    share(o_xo, HA, HA, 17)
    got(o_xo, FA, HB, 14)
    share(o_xo, FA, HB, 18)
    got(o_xo, FA + HB, HB, 15)
    share(o_xo, FA + HB, HB, 19)
    shared(n_xo, FA, HB, 7)
    shared(n_xo, FA + HB, HB, 8)
    shared(n_xo, 0, HA, 14)
    shared(n_xo, HA, HA, 15)
    forward(y * 4 + xo)
    shared(m_xo, 0, HA, 16)
    shared(m_xo, HA, HA, 17)
    shared(m_xo, FA, HB, 18)
    shared(m_xo, FA + HB, HB, 19)
    forward(yo * 4 + xo)

    keep = pltpu.make_async_copy(al, all_out, out_sem)
    keep.start()

    turned_pre = pre[...].T
    pg, pu = turned_pre[0:HID], turned_pre[HID : 2 * HID]
    sig = jax.nn.sigmoid(pg)
    act = pg * sig
    hidden = act * pu
    bk = back[...]
    gate_terms = split_gate(
        jnp.sum(bk * hidden.astype(BF).astype(F32), axis=0, keepdims=True)
    )
    dhid = gate_row * bk
    dd[0:HID, :] = (dhid * pu * sig * (1.0 + pg * (1.0 - sig))).astype(BF)
    dd[HID : 2 * HID, :] = (dhid * act).astype(BF)
    hg[...] = (hidden * gate_row).astype(BF)
    dd_out[...] = dd[...]
    hg_out[...] = hg[...]

    def term(b):
        at = pl.ds(pl.multiple_of(b * F, 16), F)
        return jnp.dot(wgu[at, :], dd[...], preferred_element_type=F32)

    order = [(yo, xo), (yo, xl), (yo, xr), (y, xo), (yo, x), (y, xl), (y, xr), (y, x)]
    ts_copies = []
    for n, (yy, xx) in enumerate(order):
        tsend[n, 0:F, :] = term(dev(yy, xx, 1 - c)).astype(BF)
        tsend[n, F:RB, :] = gate_terms
        copy = pltpu.make_async_remote_copy(
            src_ref=tsend.at[n], dst_ref=tsib.at[n],
            send_sem=ts_send.at[n], recv_sem=ts_recv.at[n],
            device_id=(me, sib), device_id_type=MESH,
        )
        copy.start()
        ts_copies.append(copy)

    def gate_total(*blocks):
        total = sum(block.astype(F32) for block in blocks)
        return jnp.sum(total, axis=0, keepdims=True)

    r_copies = []
    for n, (yy, xx) in enumerate(order):
        part = term(dev(yy, xx, c))
        ts_copies[n].wait_recv()
        part = part + tsib[n, 0:F, :].astype(F32)
        gate_part = gate_total(gate_terms, tsib[n, F:RB, :])
        if n < 7:
            rsend[n, 0:F, :] = part.astype(BF)
            rsend[n, F:RB, :] = split_gate(gate_part)
            copy = pltpu.make_async_remote_copy(
                src_ref=rsend.at[n], dst_ref=rrecv.at[n],
                send_sem=r_send.at[n], recv_sem=r_recv.at[n],
                device_id=(me, dev(yy, xx, c)), device_id_type=MESH,
            )
            copy.start()
            r_copies.append(copy)
        else:
            total, gate_sum = part, gate_part
    for n in range(6, -1, -1):
        r_copies[n].wait_recv()
        total = total + rrecv[n, 0:F, :].astype(F32)
        gate_sum = gate_sum + gate_total(rrecv[n, F:RB, :])

    rpad[0:F, :] = total.astype(BF)
    rpad[F:RB, :] = split_gate(gate_sum)
    rpad[RB:512, :] = jnp.zeros((512 - RB, SLOTS), BF)
    r = iota((256, SLOTS), 0)
    k = iota((256, SLOTS), 1)
    here = k == (r // 16) * 8 + r % 8
    low = (r % 16) < 8
    first = jnp.where(jnp.logical_and(here, low), 1.0, 0.0).astype(BF)
    other = jnp.where(jnp.logical_and(here, jnp.logical_not(low)), 1.0, 0.0).astype(BF)
    nt = (((1,), (1,)), ((), ()))
    back_rows = lax.dot_general(first, rpad[0:256, :], nt, preferred_element_type=F32)
    back_rows += lax.dot_general(other, rpad[256:512, :], nt, preferred_element_type=F32)
    retb[...] = back_rows.astype(BF).reshape(NDP, 16, 256)
    b_copies = dispatch(retb, ret, b_send, b_recv)
    for copy in b_copies:
        copy.wait_recv()
    ret_out[...] = ret[...].reshape(256, 256)

    for copy in copies_a + copies_b + sends + ts_copies + r_copies + b_copies:
        copy.wait_send()
    keep.wait()


def grad_kernel(al, dd, hg, ret, pick, gt_out, gg_out, gate_out, up_out, down_out):
    nt = (((1,), (1,)), ((), ()))
    block = al[...]
    both = lax.dot_general(block[:, 0:128], dd[...], nt, preferred_element_type=F32)
    gate_out[0] = both[:, 0:HID].astype(BF)
    up_out[0] = both[:, HID : 2 * HID].astype(BF)
    down_out[0] = lax.dot_general(
        hg[...], block[:, 128:256], nt, preferred_element_type=F32
    ).astype(BF)

    @pl.when(pl.program_id(0) == 0)
    def _():
        col = iota((TOK, 256), 1)
        is_x = (col % 16) < 8
        picks = pick[...].astype(F32)
        px = jnp.where(is_x, picks, 0.0).astype(BF)
        pd = jnp.where(is_x, 0.0, picks).astype(BF)
        rows = ret[...]
        gt_out[:, 0:FA] = jnp.dot(px, rows, preferred_element_type=F32).astype(BF)
        one = jnp.dot(pd[:, 0:128], rows[0:128], preferred_element_type=F32)
        two = jnp.dot(pd[:, 128:256], rows[128:256], preferred_element_type=F32)
        gt_out[:, FA:F] = (one + two)[:, 0:FB].astype(BF)
        gg_out[:, 0:1] = one[:, FB : FB + 1] + one[:, FB + 1 : FB + 2]
        gg_out[:, 1:2] = two[:, FB : FB + 1] + two[:, FB + 1 : FB + 2]


def per_device(tokens, cotangent, gates, expert_ids, w_gate, w_up, w_down):
    vmem = pl.BlockSpec(memory_space=pltpu.VMEM)
    anym = pl.BlockSpec(memory_space=pl.ANY)
    dma = pltpu.SemaphoreType.DMA
    ret, pick, al, dd, hg = pl.pallas_call(
        comm_kernel,
        out_shape=[
            jax.ShapeDtypeStruct((256, 256), BF),
            jax.ShapeDtypeStruct((TOK, 256), BF),
            jax.ShapeDtypeStruct((D, 256), BF),
            jax.ShapeDtypeStruct((2 * HID, SLOTS), BF),
            jax.ShapeDtypeStruct((HID, SLOTS), BF),
        ],
        in_specs=[vmem] * 4 + [anym] * 3,
        out_specs=[vmem, vmem, anym, vmem, vmem],
        scratch_shapes=[
            pltpu.VMEM((D, 2 * HID), BF),
            pltpu.VMEM((HID, D), BF),
            pltpu.VMEM((2 * TOK, 512), BF),
            pltpu.VMEM((NDP, 16, 256), BF),
            pltpu.VMEM((NDP, 16, 256), BF),
            pltpu.VMEM((NDP, 16, 256), BF),
            pltpu.VMEM((NDP, 16, 256), BF),
            pltpu.VMEM((D, 256), BF),
            pltpu.VMEM((SLOTS, 2 * HID), F32),
            pltpu.VMEM((HID, SLOTS), F32),
            pltpu.VMEM((2 * HID, SLOTS), BF),
            pltpu.VMEM((HID, SLOTS), BF),
            pltpu.VMEM((8, RB, SLOTS), BF),
            pltpu.VMEM((8, RB, SLOTS), BF),
            pltpu.VMEM((7, RB, SLOTS), BF),
            pltpu.VMEM((7, RB, SLOTS), BF),
            pltpu.VMEM((512, SLOTS), BF),
            pltpu.VMEM((NDP, 16, 256), BF),
            pltpu.VMEM((NDP, 16, 256), BF),
            dma((3,)), dma(()),
            dma((NDP,)), dma((NDP,)), dma((NDP,)), dma((NDP,)),
            dma((18,)), dma((18,)), dma((20,)), dma((20,)),
            dma((8,)), dma((8,)), dma((7,)), dma((7,)),
            dma((NDP,)), dma((NDP,)),
        ],
        compiler_params=pltpu.CompilerParams(
            collective_id=0, has_side_effects=True, vmem_limit_bytes=40 * 1024 * 1024
        ),
        name="comm",
    )(tokens, cotangent, expert_ids, gates, w_gate, w_up, w_down)

    step = 2 * C
    whole = lambda *shape: pl.BlockSpec(shape, lambda i: (0,) * len(shape))
    return pl.pallas_call(
        grad_kernel,
        grid=(D // step,),
        out_shape=[
            jax.ShapeDtypeStruct((TOK, F), BF),
            jax.ShapeDtypeStruct((TOK, 2), F32),
            jax.ShapeDtypeStruct((1, D, HID), BF),
            jax.ShapeDtypeStruct((1, D, HID), BF),
            jax.ShapeDtypeStruct((1, HID, D), BF),
        ],
        in_specs=[
            pl.BlockSpec((step, 256), lambda i: (i, 0)),
            whole(2 * HID, SLOTS),
            whole(HID, SLOTS),
            whole(256, 256),
            whole(TOK, 256),
        ],
        out_specs=[
            whole(TOK, F),
            whole(TOK, 2),
            pl.BlockSpec((1, step, HID), lambda i: (0, i, 0)),
            pl.BlockSpec((1, step, HID), lambda i: (0, i, 0)),
            pl.BlockSpec((1, HID, step), lambda i: (0, 0, i)),
        ],
        compiler_params=pltpu.CompilerParams(vmem_limit_bytes=32 * 1024 * 1024),
        name="grads",
    )(al, dd, hg, ret, pick)


def solution(mesh):
    in_specs = (
        P("dp", "expert"),
        P("dp", "expert"),
        P("dp", None),
        P("dp", None),
        P("dp", None, "expert"),
        P("dp", None, "expert"),
        P("dp", "expert", None),
    )
    out_specs = (
        P("dp", "expert"),
        P("dp", None),
        P("dp", None, "expert"),
        P("dp", None, "expert"),
        P("dp", "expert", None),
    )
    return jax.shard_map(
        per_device, mesh=mesh, in_specs=in_specs, out_specs=out_specs, check_vma=False
    )
```

```python
import functools

import jax
import jax.numpy as jnp
from jax import lax
from jax.experimental import pallas as pl
from jax.experimental.pallas import tpu as pltpu
from jax.sharding import PartitionSpec as P

MESH = pl.DeviceIdType.MESH
BF = jnp.bfloat16
F32 = jnp.float32

CAP = 8
NDP = 16
NEX = 16
F = 448
FA = 256
FB = F - FA
HB = FB // 2
HA = FA // 2
C = 2 * F
D = NEX * F
HID = 128
TOK = 128
SLOTS = NDP * CAP
RB = F + 16


def iota(shape, dim):
    return lax.broadcasted_iota(jnp.int32, shape, dim)


def split_gate(row):
    hi = row.astype(BF).astype(F32)
    lo = row - hi
    r = iota((16, row.shape[1]), 0)
    return jnp.where(r == 0, hi, jnp.where(r == 1, lo, 0.0)).astype(BF)


def comm_kernel(
    tok_hbm, cot_hbm, ids_ref, gates_ref, wg_hbm, wu_hbm, wd_hbm,
    ret_out, pick_out, all_out, dd_out, hg_out,
    wgu, wd, ext, sa, sb, ra, rb, al, pre, back, dd, hg, tsend, tsib, rsend, rrecv, rpad, retb, ret,
    w_sem, out_sem, da_send, da_recv, db_send, db_recv, g_send, g_recv, sib_send, sib_recv,
    ts_send, ts_recv, r_send, r_recv, b_send, b_recv,
):
    me = lax.axis_index("dp")
    j = lax.axis_index("expert")
    y, x, c = j // 8, (j // 2) % 4, j % 2

    def dev(yy, xx, cc):
        return yy * 8 + xx * 2 + cc

    xr, xl, xo = (x + 1) % 4, (x + 3) % 4, (x + 2) % 4
    yo = 1 - y
    sib, xp, xm, yp = dev(y, x, 1 - c), dev(y, xr, c), dev(y, xl, c), dev(yo, x, c)

    started = []

    barrier = pltpu.get_barrier_semaphore()
    for i in range(1, NDP):
        pl.semaphore_signal(barrier, inc=1, device_id=((me + i) % NDP, j), device_id_type=MESH)
    chips = [(yy, xx) for yy in (y, yo) for xx in (x, xr, xl, xo)][1:]
    for yy, xx in chips:
        pl.semaphore_signal(barrier, inc=1, device_id=(me, dev(yy, xx, c)), device_id_type=MESH)
    pl.semaphore_signal(barrier, inc=1, device_id=(me, sib), device_id_type=MESH)

    loads = [
        pltpu.make_async_copy(wg_hbm.at[0], wgu.at[:, 0:HID], w_sem.at[0]),
        pltpu.make_async_copy(wu_hbm.at[0], wgu.at[:, HID : 2 * HID], w_sem.at[1]),
        pltpu.make_async_copy(wd_hbm.at[0], wd, w_sem.at[2]),
    ]
    acts = [
        pltpu.make_async_copy(tok_hbm, ext.at[0:F, 0:TOK], w_sem.at[3]),
        pltpu.make_async_copy(cot_hbm, ext.at[0:F, TOK : 2 * TOK], w_sem.at[4]),
    ]
    for load in acts + loads:
        load.start()

    row = iota((256, TOK), 0)
    chosen = jnp.where(row < 128, ids_ref[0:1, :], ids_ref[1:2, :])
    member = chosen == row // 16
    tri = (iota((TOK, TOK), 0) < iota((TOK, TOK), 1)).astype(F32).astype(BF)
    before = jnp.dot(member.astype(F32).astype(BF), tri, preferred_element_type=F32)
    pick = jnp.where(
        jnp.logical_and(member, before == (row % 8).astype(F32)), 1.0, 0.0
    )
    is_x = (row % 16) < 8
    pick_out[...] = pick.astype(BF)
    pick2 = jnp.concatenate(
        [jnp.where(is_x, pick, 0.0), jnp.where(is_x, 0.0, pick)], axis=1
    ).astype(BF)
    gates = gates_ref[...].astype(F32)
    line = iota((512 - F, TOK), 0)
    ext[F:512, 0:TOK] = jnp.where(
        line == 0, gates[0:1, :], jnp.where(line == 1, gates[1:2, :], 0.0)
    ).astype(BF)
    ext[F:512, TOK : 2 * TOK] = jnp.zeros((512 - F, TOK), BF)
    for load in acts:
        load.wait()
    slots = lax.dot_general(
        pick2, ext[...], (((1,), (1,)), ((), ())), preferred_element_type=F32
    ).astype(BF)
    sa[...] = slots[:, 0:256].reshape(NDP, 16, 256)
    sb[...] = slots[:, 256:512].reshape(NDP, 16, 256)

    pl.semaphore_wait(barrier, NDP - 1 + len(chips) + 1)

    def dispatch(src, dst, send, recv):
        copies = []
        for i in range(1, NDP):
            to = (me + i) % NDP
            copy = pltpu.make_async_remote_copy(
                src_ref=src.at[to], dst_ref=dst.at[me],
                send_sem=send.at[i], recv_sem=recv.at[i],
                device_id=(to, j), device_id_type=MESH,
            )
            copy.start()
            copies.append(copy)
            started.append(copy)
        dst[pl.ds(me, 1)] = src[pl.ds(me, 1)]
        return copies

    copies_a = dispatch(sa, ra, da_send, da_recv)
    copies_b = dispatch(sb, rb, db_send, db_recv)

    r = iota((256, 256), 0)
    k = iota((256, 256), 1)
    kk = k % 128
    perm = jnp.where(r == (kk // 8) * 16 + (k // 128) * 8 + kk % 8, 1.0, 0.0).astype(BF)

    def turned(buf):
        return lax.dot_general(
            buf[...].reshape(256, 256), perm, (((0,), (0,)), ((), ())),
            preferred_element_type=F32,
        )

    def rows(b, lo, n):
        return al.at[pl.ds(pl.multiple_of(b * F + lo, 16), n)]

    def push(b, lo, n, to, s):
        copy = pltpu.make_async_remote_copy(
            src_ref=rows(b, lo, n), dst_ref=rows(b, lo, n),
            send_sem=g_send.at[s], recv_sem=g_recv.at[s],
            device_id=(me, to), device_id_type=MESH,
        )
        copy.start()
        started.append(copy)

    def share(b, lo, n, s):
        copy = pltpu.make_async_remote_copy(
            src_ref=rows(b, lo, n), dst_ref=rows(b, lo, n),
            send_sem=sib_send.at[s], recv_sem=sib_recv.at[s],
            device_id=(me, sib), device_id_type=MESH,
        )
        copy.start()
        started.append(copy)

    def got(b, lo, n, s):
        pltpu.make_async_remote_copy(
            src_ref=rows(b, lo, n), dst_ref=rows(b, lo, n),
            send_sem=g_send.at[s], recv_sem=g_recv.at[s],
            device_id=(me, sib), device_id_type=MESH,
        ).wait_recv()

    def shared(b, lo, n, s):
        pltpu.make_async_remote_copy(
            src_ref=rows(b, lo, n), dst_ref=rows(b, lo, n),
            send_sem=sib_send.at[s], recv_sem=sib_recv.at[s],
            device_id=(me, sib), device_id_type=MESH,
        ).wait_recv()

    b_own, b_xr, b_xl, b_xo = (dev(y, xx, c) for xx in (x, xr, xl, xo))
    o_own, o_xr, o_xl, o_xo = (dev(yo, xx, c) for xx in (x, xr, xl, xo))

    for copy in copies_a:
        copy.wait_recv()
    al[pl.ds(pl.multiple_of(j * F, 16), FA), :] = turned(ra).astype(BF)
    push(b_own, 0, FA, yp, 0)
    push(b_own, 0, FA, xp, 1)
    push(b_own, 0, FA, xm, 2)
    share(b_own, 0, FA, 0)

    for copy in copies_b:
        copy.wait_recv()
    second = turned(rb)
    al[pl.ds(pl.multiple_of(j * F + FA, 16), FB), :] = second[0:FB].astype(BF)
    gate_row = jnp.where(me < NDP // 2, second[FB : FB + 1, 0:128], second[FB + 1 : FB + 2, 0:128])
    push(b_own, FA, FB, yp, 3)
    push(b_own, FA, FB, xp, 4)
    push(b_own, FA, FB, xm, 5)
    share(b_own, FA, FB, 1)

    pre[...] = jnp.zeros_like(pre)
    back[...] = jnp.zeros_like(back)
    for load in loads:
        load.wait()

    def forward(chip):
        at = pl.ds(pl.multiple_of(chip * C, 128), C)
        block = al[at, :]
        pre[...] += lax.dot_general(
            block[:, 0:128], wgu[at, :], (((0,), (0,)), ((), ())), preferred_element_type=F32
        )
        back[...] += jnp.dot(wd[:, at], block[:, 128:256], preferred_element_type=F32)

    got(o_own, 0, FA, 0)
    push(o_own, 0, FA, xp, 6)
    push(o_own, 0, FA, xm, 7)
    share(o_own, 0, FA, 2)
    got(b_xl, FA, FB, 4)
    push(b_xl, FA, HB, xp, 8)
    push(b_xl, FA, FB, yp, 9)
    share(b_xl, FA, FB, 3)
    got(b_xr, FA, FB, 5)
    push(b_xr, FA + HB, HB, xm, 10)
    push(b_xr, FA, FB, yp, 11)
    share(b_xr, FA, FB, 4)
    got(b_xl, 0, FA, 1)
    push(b_xl, 0, HA, xp, 12)
    share(b_xl, 0, FA, 5)
    got(b_xr, 0, FA, 2)
    push(b_xr, HA, HA, xm, 13)
    share(b_xr, 0, FA, 6)

    sib_own = dev(y, x, 1 - c)
    shared(sib_own, 0, FA, 0)
    shared(sib_own, FA, FB, 1)
    forward(y * 4 + x)

    got(b_xo, FA, HB, 8)
    push(b_xo, FA, HB, yp, 14)
    share(b_xo, FA, HB, 7)
    got(b_xo, FA + HB, HB, 10)
    push(b_xo, FA + HB, HB, yp, 15)
    share(b_xo, FA + HB, HB, 8)
    got(o_xl, 0, FA, 6)
    push(o_xl, 0, HA, xp, 16)
    share(o_xl, 0, FA, 9)
    got(o_xr, 0, FA, 7)
    push(o_xr, HA, HA, xm, 17)
    share(o_xr, 0, FA, 10)
    got(o_own, FA, FB, 3)
    share(o_own, FA, FB, 11)

    n_xr, n_xl, n_xo = (dev(y, xx, 1 - c) for xx in (xr, xl, xo))
    m_own, m_xr, m_xl, m_xo = (dev(yo, xx, 1 - c) for xx in (x, xr, xl, xo))
    shared(n_xl, FA, FB, 3)
    shared(n_xl, 0, FA, 5)
    forward(y * 4 + xl)
    got(o_xl, FA, FB, 9)
    share(o_xl, FA, FB, 12)
    shared(n_xr, FA, FB, 4)
    shared(n_xr, 0, FA, 6)
    forward(y * 4 + xr)
    got(o_xr, FA, FB, 11)
    share(o_xr, FA, FB, 13)
    shared(m_own, 0, FA, 2)
    shared(m_own, FA, FB, 11)
    forward(yo * 4 + x)
    got(b_xo, 0, HA, 12)
    share(b_xo, 0, HA, 14)
    got(b_xo, HA, HA, 13)
    share(b_xo, HA, HA, 15)
    shared(m_xl, 0, FA, 9)
    shared(m_xl, FA, FB, 12)
    forward(yo * 4 + xl)
    shared(m_xr, 0, FA, 10)
    shared(m_xr, FA, FB, 13)
    forward(yo * 4 + xr)
    got(o_xo, 0, HA, 16)
    share(o_xo, 0, HA, 16)
    got(o_xo, HA, HA, 17)
    share(o_xo, HA, HA, 17)
    got(o_xo, FA, HB, 14)
    share(o_xo, FA, HB, 18)
    got(o_xo, FA + HB, HB, 15)
    share(o_xo, FA + HB, HB, 19)
    shared(n_xo, FA, HB, 7)
    shared(n_xo, FA + HB, HB, 8)
    shared(n_xo, 0, HA, 14)
    shared(n_xo, HA, HA, 15)
    forward(y * 4 + xo)
    shared(m_xo, 0, HA, 16)
    shared(m_xo, HA, HA, 17)
    shared(m_xo, FA, HB, 18)
    shared(m_xo, FA + HB, HB, 19)
    forward(yo * 4 + xo)

    keep = pltpu.make_async_copy(al, all_out, out_sem)
    keep.start()

    turned_pre = pre[...].T
    pg, pu = turned_pre[0:HID], turned_pre[HID : 2 * HID]
    sig = jax.nn.sigmoid(pg)
    act = pg * sig
    hidden = act * pu
    bk = back[...]
    gate_terms = split_gate(
        jnp.sum(bk * hidden.astype(BF).astype(F32), axis=0, keepdims=True)
    )
    dhid = gate_row * bk
    dd[0:HID, :] = (dhid * pu * sig * (1.0 + pg * (1.0 - sig))).astype(BF)
    dd[HID : 2 * HID, :] = (dhid * act).astype(BF)
    hg[...] = (hidden * gate_row).astype(BF)
    dd_out[...] = dd[...]
    hg_out[...] = hg[...]

    def term(b):
        at = pl.ds(pl.multiple_of(b * F, 16), F)
        return jnp.dot(wgu[at, :], dd[...], preferred_element_type=F32)

    order = [(yo, xo), (yo, xl), (yo, xr), (y, xo), (yo, x), (y, xl), (y, xr), (y, x)]
    ts_copies = []
    for n, (yy, xx) in enumerate(order):
        tsend[n, 0:F, :] = term(dev(yy, xx, 1 - c)).astype(BF)
        tsend[n, F:RB, :] = gate_terms
        copy = pltpu.make_async_remote_copy(
            src_ref=tsend.at[n], dst_ref=tsib.at[n],
            send_sem=ts_send.at[n], recv_sem=ts_recv.at[n],
            device_id=(me, sib), device_id_type=MESH,
        )
        copy.start()
        ts_copies.append(copy)
        started.append(copy)

    def gate_total(*blocks):
        total = sum(block.astype(F32) for block in blocks)
        return jnp.sum(total, axis=0, keepdims=True)

    r_copies = []
    for n, (yy, xx) in enumerate(order):
        part = term(dev(yy, xx, c))
        ts_copies[n].wait_recv()
        part = part + tsib[n, 0:F, :].astype(F32)
        gate_part = gate_total(gate_terms, tsib[n, F:RB, :])
        if n < 7:
            rsend[n, 0:F, :] = part.astype(BF)
            rsend[n, F:RB, :] = split_gate(gate_part)
            copy = pltpu.make_async_remote_copy(
                src_ref=rsend.at[n], dst_ref=rrecv.at[n],
                send_sem=r_send.at[n], recv_sem=r_recv.at[n],
                device_id=(me, dev(yy, xx, c)), device_id_type=MESH,
            )
            copy.start()
            r_copies.append(copy)
            started.append(copy)
        else:
            total, gate_sum = part, gate_part
    for n in range(6, -1, -1):
        r_copies[n].wait_recv()
        total = total + rrecv[n, 0:F, :].astype(F32)
        gate_sum = gate_sum + gate_total(rrecv[n, F:RB, :])

    rpad[0:F, :] = total.astype(BF)
    rpad[F:RB, :] = split_gate(gate_sum)
    rpad[RB:512, :] = jnp.zeros((512 - RB, SLOTS), BF)
    r = iota((256, SLOTS), 0)
    k = iota((256, SLOTS), 1)
    here = k == (r // 16) * 8 + r % 8
    low = (r % 16) < 8
    first = jnp.where(jnp.logical_and(here, low), 1.0, 0.0).astype(BF)
    other = jnp.where(jnp.logical_and(here, jnp.logical_not(low)), 1.0, 0.0).astype(BF)
    nt = (((1,), (1,)), ((), ()))
    back_rows = lax.dot_general(first, rpad[0:256, :], nt, preferred_element_type=F32)
    back_rows += lax.dot_general(other, rpad[256:512, :], nt, preferred_element_type=F32)
    retb[...] = back_rows.astype(BF).reshape(NDP, 16, 256)
    b_copies = dispatch(retb, ret, b_send, b_recv)
    for copy in b_copies:
        copy.wait_recv()
    ret_out[...] = ret[...].reshape(256, 256)

    for copy in started:
        copy.wait_send()
    keep.wait()


def grad_kernel(al, dd, hg, ret, pick, gt_out, gg_out, gate_out, up_out, down_out):
    nt = (((1,), (1,)), ((), ()))
    block = al[...]
    both = lax.dot_general(block[:, 0:128], dd[...], nt, preferred_element_type=F32)
    gate_out[0] = both[:, 0:HID].astype(BF)
    up_out[0] = both[:, HID : 2 * HID].astype(BF)
    down_out[0] = lax.dot_general(
        hg[...], block[:, 128:256], nt, preferred_element_type=F32
    ).astype(BF)

    @pl.when(pl.program_id(0) == 0)
    def _():
        tn = (((0,), (0,)), ((), ()))
        is_x = (iota((256, TOK), 0) % 16) < 8
        picks = pick[...].astype(F32)
        px = jnp.where(is_x, picks, 0.0).astype(BF)
        pd = jnp.where(is_x, 0.0, picks).astype(BF)
        rows = ret[...]
        gt_out[0:FA, :] = lax.dot_general(rows, px, tn, preferred_element_type=F32).astype(BF)
        one = lax.dot_general(rows[0:128], pd[0:128], tn, preferred_element_type=F32)
        two = lax.dot_general(rows[128:256], pd[128:256], tn, preferred_element_type=F32)
        gt_out[FA:F, :] = (one + two)[0:FB].astype(BF)
        gg_out[0:1, :] = one[FB : FB + 1] + one[FB + 1 : FB + 2]
        gg_out[1:2, :] = two[FB : FB + 1] + two[FB + 1 : FB + 2]


def per_device(tokens, cotangent, gates, expert_ids, w_gate, w_up, w_down):
    vmem = pl.BlockSpec(memory_space=pltpu.VMEM)
    anym = pl.BlockSpec(memory_space=pl.ANY)
    hbm = pl.BlockSpec(memory_space=pltpu.HBM)
    dma = pltpu.SemaphoreType.DMA
    ret, pick, al, dd, hg = pl.pallas_call(
        comm_kernel,
        out_shape=[
            jax.ShapeDtypeStruct((256, 256), BF),
            jax.ShapeDtypeStruct((256, TOK), BF),
            jax.ShapeDtypeStruct((D, 256), BF),
            jax.ShapeDtypeStruct((2 * HID, SLOTS), BF),
            jax.ShapeDtypeStruct((HID, SLOTS), BF),
        ],
        in_specs=[hbm] * 2 + [vmem] * 2 + [hbm] * 3,
        out_specs=[vmem, vmem, anym, vmem, vmem],
        scratch_shapes=[
            pltpu.VMEM((D, 2 * HID), BF),
            pltpu.VMEM((HID, D), BF),
            pltpu.VMEM((512, 2 * TOK), BF),
            pltpu.VMEM((NDP, 16, 256), BF),
            pltpu.VMEM((NDP, 16, 256), BF),
            pltpu.VMEM((NDP, 16, 256), BF),
            pltpu.VMEM((NDP, 16, 256), BF),
            pltpu.VMEM((D, 256), BF),
            pltpu.VMEM((SLOTS, 2 * HID), F32),
            pltpu.VMEM((HID, SLOTS), F32),
            pltpu.VMEM((2 * HID, SLOTS), BF),
            pltpu.VMEM((HID, SLOTS), BF),
            pltpu.VMEM((8, RB, SLOTS), BF),
            pltpu.VMEM((8, RB, SLOTS), BF),
            pltpu.VMEM((7, RB, SLOTS), BF),
            pltpu.VMEM((7, RB, SLOTS), BF),
            pltpu.VMEM((512, SLOTS), BF),
            pltpu.VMEM((NDP, 16, 256), BF),
            pltpu.VMEM((NDP, 16, 256), BF),
            dma((5,)), dma(()),
            dma((NDP,)), dma((NDP,)), dma((NDP,)), dma((NDP,)),
            dma((18,)), dma((18,)), dma((20,)), dma((20,)),
            dma((8,)), dma((8,)), dma((7,)), dma((7,)),
            dma((NDP,)), dma((NDP,)),
        ],
        compiler_params=pltpu.CompilerParams(
            collective_id=0, has_side_effects=True, vmem_limit_bytes=58 * 1024 * 1024
        ),
        name="comm",
    )(tokens.T, cotangent.T, expert_ids.T, gates.T, w_gate, w_up, w_down)

    step = 2 * C
    whole = lambda *shape: pl.BlockSpec(shape, lambda i: (0,) * len(shape))
    gt, gg, gate, up, down = pl.pallas_call(
        grad_kernel,
        grid=(D // step,),
        out_shape=[
            jax.ShapeDtypeStruct((F, TOK), BF),
            jax.ShapeDtypeStruct((2, TOK), F32),
            jax.ShapeDtypeStruct((1, D, HID), BF),
            jax.ShapeDtypeStruct((1, D, HID), BF),
            jax.ShapeDtypeStruct((1, HID, D), BF),
        ],
        in_specs=[
            pl.BlockSpec((step, 256), lambda i: (i, 0)),
            whole(2 * HID, SLOTS),
            whole(HID, SLOTS),
            whole(256, 256),
            whole(256, TOK),
        ],
        out_specs=[
            whole(F, TOK),
            whole(2, TOK),
            pl.BlockSpec((1, step, HID), lambda i: (0, i, 0)),
            pl.BlockSpec((1, step, HID), lambda i: (0, i, 0)),
            pl.BlockSpec((1, HID, step), lambda i: (0, 0, i)),
        ],
        compiler_params=pltpu.CompilerParams(vmem_limit_bytes=58 * 1024 * 1024),
        name="grads",
    )(al, dd, hg, ret, pick)
    return gt.T, gg.T, gate, up, down


def solution(mesh):
    in_specs = (
        P("dp", "expert"),
        P("dp", "expert"),
        P("dp", None),
        P("dp", None),
        P("dp", None, "expert"),
        P("dp", None, "expert"),
        P("dp", "expert", None),
    )
    out_specs = (
        P("dp", "expert"),
        P("dp", None),
        P("dp", None, "expert"),
        P("dp", None, "expert"),
        P("dp", "expert", None),
    )
    return jax.shard_map(
        per_device, mesh=mesh, in_specs=in_specs, out_specs=out_specs, check_vma=False
    )
```

```python
import functools

import jax
import jax.numpy as jnp
from jax import lax
from jax.experimental import pallas as pl
from jax.experimental.pallas import tpu as pltpu
from jax.sharding import PartitionSpec as P

MESH = pl.DeviceIdType.MESH
BF = jnp.bfloat16
F32 = jnp.float32

CAP = 8
NDP = 16
NEX = 16
F = 448
FA = 256
FB = F - FA
HB = FB // 2
HA = FA // 2
C = 2 * F
D = NEX * F
HID = 128
TOK = 128
SLOTS = NDP * CAP
FAR_FIRST = (7, 9, 8, 5, 6, 10, 11, 3, 13, 4, 12, 1, 15, 2, 14)
RB = F + 16


def iota(shape, dim):
    return lax.broadcasted_iota(jnp.int32, shape, dim)


def split_gate(row):
    hi = row.astype(BF).astype(F32)
    lo = row - hi
    r = iota((16, row.shape[1]), 0)
    return jnp.where(r == 0, hi, jnp.where(r == 1, lo, 0.0)).astype(BF)


def comm_kernel(
    tok_hbm, cot_hbm, ids_hbm, gates_hbm, wg_hbm, wu_hbm, wd_hbm,
    ret_out, pick_out, gate_out, up_out, down_out,
    ids_ref, gates_ref, wgu, wd, ext, sa, sb, ra, rb, al, pre, back, dd, hg, tsend, tsib, rsend, rrecv, rpad, retb, ret,
    w_sem, da_send, da_recv, db_send, db_recv, g_send, g_recv, sib_send, sib_recv,
    ts_send, ts_recv, r_send, r_recv, b_send, b_recv,
):
    me = lax.axis_index("dp")
    j = lax.axis_index("expert")
    y, x, c = j // 8, (j // 2) % 4, j % 2

    def dev(yy, xx, cc):
        return yy * 8 + xx * 2 + cc

    xr, xl, xo = (x + 1) % 4, (x + 3) % 4, (x + 2) % 4
    yo = 1 - y
    sib, xp, xm, yp = dev(y, x, 1 - c), dev(y, xr, c), dev(y, xl, c), dev(yo, x, c)

    started = []

    barrier = pltpu.get_barrier_semaphore()
    for i in FAR_FIRST:
        pl.semaphore_signal(barrier, inc=1, device_id=((me + i) % NDP, j), device_id_type=MESH)
    chips = [(yy, xx) for yy in (y, yo) for xx in (x, xr, xl, xo)][1:]
    for yy, xx in chips:
        pl.semaphore_signal(barrier, inc=1, device_id=(me, dev(yy, xx, c)), device_id_type=MESH)
    pl.semaphore_signal(barrier, inc=1, device_id=(me, sib), device_id_type=MESH)

    loads = [
        pltpu.make_async_copy(wg_hbm.at[0], wgu.at[:, 0:HID], w_sem.at[0]),
        pltpu.make_async_copy(wu_hbm.at[0], wgu.at[:, HID : 2 * HID], w_sem.at[1]),
        pltpu.make_async_copy(wd_hbm.at[0], wd, w_sem.at[2]),
    ]
    acts = [
        pltpu.make_async_copy(ids_hbm, ids_ref, w_sem.at[5]),
        pltpu.make_async_copy(gates_hbm, gates_ref, w_sem.at[6]),
        pltpu.make_async_copy(tok_hbm, ext.at[0:F, 0:TOK], w_sem.at[3]),
        pltpu.make_async_copy(cot_hbm, ext.at[0:F, TOK : 2 * TOK], w_sem.at[4]),
    ]
    for load in acts + loads:
        load.start()
    acts[0].wait()
    acts[1].wait()

    row = iota((256, TOK), 0)
    chosen = jnp.where(row < 128, ids_ref[0:1, :], ids_ref[1:2, :])
    member = chosen == row // 16
    tri = (iota((TOK, TOK), 0) < iota((TOK, TOK), 1)).astype(F32).astype(BF)
    before = jnp.dot(member.astype(F32).astype(BF), tri, preferred_element_type=F32)
    pick = jnp.where(
        jnp.logical_and(member, before == (row % 8).astype(F32)), 1.0, 0.0
    )
    is_x = (row % 16) < 8
    pick_out[...] = pick.astype(BF)
    pick2 = jnp.concatenate(
        [jnp.where(is_x, pick, 0.0), jnp.where(is_x, 0.0, pick)], axis=1
    ).astype(BF)
    gates = gates_ref[...].astype(F32)
    line = iota((512 - F, TOK), 0)
    ext[F:512, 0:TOK] = jnp.where(
        line == 0, gates[0:1, :], jnp.where(line == 1, gates[1:2, :], 0.0)
    ).astype(BF)
    ext[F:512, TOK : 2 * TOK] = jnp.zeros((512 - F, TOK), BF)
    for load in acts[2:]:
        load.wait()
    slots = lax.dot_general(
        pick2, ext[...], (((1,), (1,)), ((), ())), preferred_element_type=F32
    ).astype(BF)
    sa[...] = slots[:, 0:256].reshape(NDP, 16, 256)
    sb[...] = slots[:, 256:512].reshape(NDP, 16, 256)

    pl.semaphore_wait(barrier, NDP - 1 + len(chips) + 1)

    def dispatch(src, dst, send, recv):
        copies = []
        for i in FAR_FIRST:
            to = (me + i) % NDP
            copy = pltpu.make_async_remote_copy(
                src_ref=src.at[to], dst_ref=dst.at[me],
                send_sem=send.at[i], recv_sem=recv.at[i],
                device_id=(to, j), device_id_type=MESH,
            )
            copy.start()
            copies.append(copy)
            started.append(copy)
        dst[pl.ds(me, 1)] = src[pl.ds(me, 1)]
        return copies

    copies_a = dispatch(sa, ra, da_send, da_recv)
    copies_b = dispatch(sb, rb, db_send, db_recv)

    r = iota((256, 256), 0)
    k = iota((256, 256), 1)
    kk = k % 128
    perm = jnp.where(r == (kk // 8) * 16 + (k // 128) * 8 + kk % 8, 1.0, 0.0).astype(BF)

    def turned(buf):
        return lax.dot_general(
            buf[...].reshape(256, 256), perm, (((0,), (0,)), ((), ())),
            preferred_element_type=F32,
        )

    def rows(b, lo, n):
        return al.at[pl.ds(pl.multiple_of(b * F + lo, 16), n)]

    def push(b, lo, n, to, s):
        copy = pltpu.make_async_remote_copy(
            src_ref=rows(b, lo, n), dst_ref=rows(b, lo, n),
            send_sem=g_send.at[s], recv_sem=g_recv.at[s],
            device_id=(me, to), device_id_type=MESH,
        )
        copy.start()
        started.append(copy)

    def share(b, lo, n, s):
        copy = pltpu.make_async_remote_copy(
            src_ref=rows(b, lo, n), dst_ref=rows(b, lo, n),
            send_sem=sib_send.at[s], recv_sem=sib_recv.at[s],
            device_id=(me, sib), device_id_type=MESH,
        )
        copy.start()
        started.append(copy)

    def got(b, lo, n, s):
        pltpu.make_async_remote_copy(
            src_ref=rows(b, lo, n), dst_ref=rows(b, lo, n),
            send_sem=g_send.at[s], recv_sem=g_recv.at[s],
            device_id=(me, sib), device_id_type=MESH,
        ).wait_recv()

    def shared(b, lo, n, s):
        pltpu.make_async_remote_copy(
            src_ref=rows(b, lo, n), dst_ref=rows(b, lo, n),
            send_sem=sib_send.at[s], recv_sem=sib_recv.at[s],
            device_id=(me, sib), device_id_type=MESH,
        ).wait_recv()

    b_own, b_xr, b_xl, b_xo = (dev(y, xx, c) for xx in (x, xr, xl, xo))
    o_own, o_xr, o_xl, o_xo = (dev(yo, xx, c) for xx in (x, xr, xl, xo))

    for copy in copies_a:
        copy.wait_recv()
    al[pl.ds(pl.multiple_of(j * F, 16), FA), :] = turned(ra).astype(BF)
    push(b_own, 0, FA, yp, 0)
    push(b_own, 0, FA, xp, 1)
    push(b_own, 0, FA, xm, 2)
    share(b_own, 0, FA, 0)

    for copy in copies_b:
        copy.wait_recv()
    second = turned(rb)
    al[pl.ds(pl.multiple_of(j * F + FA, 16), FB), :] = second[0:FB].astype(BF)
    gate_row = jnp.where(me < NDP // 2, second[FB : FB + 1, 0:128], second[FB + 1 : FB + 2, 0:128])
    push(b_own, FA, FB, yp, 3)
    push(b_own, FA, FB, xp, 4)
    push(b_own, FA, FB, xm, 5)
    share(b_own, FA, FB, 1)

    pre[...] = jnp.zeros_like(pre)
    back[...] = jnp.zeros_like(back)
    for load in loads:
        load.wait()

    def forward(chip):
        at = pl.ds(pl.multiple_of(chip * C, 128), C)
        block = al[at, :]
        pre[...] += lax.dot_general(
            block[:, 0:128], wgu[at, :], (((0,), (0,)), ((), ())), preferred_element_type=F32
        )
        back[...] += jnp.dot(wd[:, at], block[:, 128:256], preferred_element_type=F32)

    got(o_own, 0, FA, 0)
    push(o_own, 0, FA, xp, 6)
    push(o_own, 0, FA, xm, 7)
    share(o_own, 0, FA, 2)
    got(b_xl, FA, FB, 4)
    push(b_xl, FA, HB, xp, 8)
    push(b_xl, FA, FB, yp, 9)
    share(b_xl, FA, FB, 3)
    got(b_xr, FA, FB, 5)
    push(b_xr, FA + HB, HB, xm, 10)
    push(b_xr, FA, FB, yp, 11)
    share(b_xr, FA, FB, 4)
    got(b_xl, 0, FA, 1)
    push(b_xl, 0, HA, xp, 12)
    share(b_xl, 0, FA, 5)
    got(b_xr, 0, FA, 2)
    push(b_xr, HA, HA, xm, 13)
    share(b_xr, 0, FA, 6)

    sib_own = dev(y, x, 1 - c)
    shared(sib_own, 0, FA, 0)
    shared(sib_own, FA, FB, 1)
    forward(y * 4 + x)

    got(b_xo, FA, HB, 8)
    push(b_xo, FA, HB, yp, 14)
    share(b_xo, FA, HB, 7)
    got(b_xo, FA + HB, HB, 10)
    push(b_xo, FA + HB, HB, yp, 15)
    share(b_xo, FA + HB, HB, 8)
    got(o_xl, 0, FA, 6)
    push(o_xl, 0, HA, xp, 16)
    share(o_xl, 0, FA, 9)
    got(o_xr, 0, FA, 7)
    push(o_xr, HA, HA, xm, 17)
    share(o_xr, 0, FA, 10)
    got(o_own, FA, FB, 3)
    share(o_own, FA, FB, 11)

    n_xr, n_xl, n_xo = (dev(y, xx, 1 - c) for xx in (xr, xl, xo))
    m_own, m_xr, m_xl, m_xo = (dev(yo, xx, 1 - c) for xx in (x, xr, xl, xo))
    shared(n_xl, FA, FB, 3)
    shared(n_xl, 0, FA, 5)
    forward(y * 4 + xl)
    got(o_xl, FA, FB, 9)
    share(o_xl, FA, FB, 12)
    shared(n_xr, FA, FB, 4)
    shared(n_xr, 0, FA, 6)
    forward(y * 4 + xr)
    got(o_xr, FA, FB, 11)
    share(o_xr, FA, FB, 13)
    shared(m_own, 0, FA, 2)
    shared(m_own, FA, FB, 11)
    forward(yo * 4 + x)
    got(b_xo, 0, HA, 12)
    share(b_xo, 0, HA, 14)
    got(b_xo, HA, HA, 13)
    share(b_xo, HA, HA, 15)
    shared(m_xl, 0, FA, 9)
    shared(m_xl, FA, FB, 12)
    forward(yo * 4 + xl)
    shared(m_xr, 0, FA, 10)
    shared(m_xr, FA, FB, 13)
    forward(yo * 4 + xr)
    got(o_xo, 0, HA, 16)
    share(o_xo, 0, HA, 16)
    got(o_xo, HA, HA, 17)
    share(o_xo, HA, HA, 17)
    got(o_xo, FA, HB, 14)
    share(o_xo, FA, HB, 18)
    got(o_xo, FA + HB, HB, 15)
    share(o_xo, FA + HB, HB, 19)
    shared(n_xo, FA, HB, 7)
    shared(n_xo, FA + HB, HB, 8)
    shared(n_xo, 0, HA, 14)
    shared(n_xo, HA, HA, 15)
    forward(y * 4 + xo)
    shared(m_xo, 0, HA, 16)
    shared(m_xo, HA, HA, 17)
    shared(m_xo, FA, HB, 18)
    shared(m_xo, FA + HB, HB, 19)
    forward(yo * 4 + xo)

    turned_pre = pre[...].T
    pg, pu = turned_pre[0:HID], turned_pre[HID : 2 * HID]
    sig = jax.nn.sigmoid(pg)
    act = pg * sig
    hidden = act * pu
    bk = back[...]
    gate_terms = split_gate(
        jnp.sum(bk * hidden.astype(BF).astype(F32), axis=0, keepdims=True)
    )
    dhid = gate_row * bk
    dd[0:HID, :] = (dhid * pu * sig * (1.0 + pg * (1.0 - sig))).astype(BF)
    dd[HID : 2 * HID, :] = (dhid * act).astype(BF)
    hg[...] = (hidden * gate_row).astype(BF)

    nt = (((1,), (1,)), ((), ()))

    def term(b):
        at = pl.ds(pl.multiple_of(b * F, 16), F)
        return jnp.dot(wgu[at, :], dd[...], preferred_element_type=F32)

    order = [(yo, xo), (yo, xl), (yo, xr), (y, xo), (yo, x), (y, xl), (y, xr), (y, x)]
    ts_copies = []
    for n, (yy, xx) in enumerate(order):
        tsend[n, 0:F, :] = term(dev(yy, xx, 1 - c)).astype(BF)
        tsend[n, F:RB, :] = gate_terms
        copy = pltpu.make_async_remote_copy(
            src_ref=tsend.at[n], dst_ref=tsib.at[n],
            send_sem=ts_send.at[n], recv_sem=ts_recv.at[n],
            device_id=(me, sib), device_id_type=MESH,
        )
        copy.start()
        ts_copies.append(copy)
        started.append(copy)

    def gate_total(*blocks):
        total = sum(block.astype(F32) for block in blocks)
        return jnp.sum(total, axis=0, keepdims=True)

    r_copies = []
    for n, (yy, xx) in enumerate(order):
        part = term(dev(yy, xx, c))
        ts_copies[n].wait_recv()
        part = part + tsib[n, 0:F, :].astype(F32)
        gate_part = gate_total(gate_terms, tsib[n, F:RB, :])
        if n < 7:
            rsend[n, 0:F, :] = part.astype(BF)
            rsend[n, F:RB, :] = split_gate(gate_part)
            copy = pltpu.make_async_remote_copy(
                src_ref=rsend.at[n], dst_ref=rrecv.at[n],
                send_sem=r_send.at[n], recv_sem=r_recv.at[n],
                device_id=(me, dev(yy, xx, c)), device_id_type=MESH,
            )
            copy.start()
            r_copies.append(copy)
            started.append(copy)
        else:
            total, gate_sum = part, gate_part

    def grads(i, carry):
        at = pl.ds(pl.multiple_of(i * C, 128), C)
        block = al[at, :]
        both = lax.dot_general(block[:, 0:128], dd[...], nt, preferred_element_type=F32)
        gate_out[at, :] = both[:, 0:HID].astype(BF)
        up_out[at, :] = both[:, HID : 2 * HID].astype(BF)
        down_out[:, at] = lax.dot_general(
            hg[...], block[:, 128:256], nt, preferred_element_type=F32
        ).astype(BF)
        return carry

    lax.fori_loop(0, D // C, grads, 0)

    for n in range(6, -1, -1):
        r_copies[n].wait_recv()
        total = total + rrecv[n, 0:F, :].astype(F32)
        gate_sum = gate_sum + gate_total(rrecv[n, F:RB, :])

    rpad[0:F, :] = total.astype(BF)
    rpad[F:RB, :] = split_gate(gate_sum)
    rpad[RB:512, :] = jnp.zeros((512 - RB, SLOTS), BF)
    r = iota((256, SLOTS), 0)
    k = iota((256, SLOTS), 1)
    here = k == (r // 16) * 8 + r % 8
    low = (r % 16) < 8
    first = jnp.where(jnp.logical_and(here, low), 1.0, 0.0).astype(BF)
    other = jnp.where(jnp.logical_and(here, jnp.logical_not(low)), 1.0, 0.0).astype(BF)
    nt = (((1,), (1,)), ((), ()))
    back_rows = lax.dot_general(first, rpad[0:256, :], nt, preferred_element_type=F32)
    back_rows += lax.dot_general(other, rpad[256:512, :], nt, preferred_element_type=F32)
    retb[...] = back_rows.astype(BF).reshape(NDP, 16, 256)
    b_copies = dispatch(retb, ret, b_send, b_recv)
    for copy in b_copies:
        copy.wait_recv()
    ret_out[...] = ret[...].reshape(256, 256)

    for copy in started:
        copy.wait_send()


def finish_kernel(ret, pick, gate, up, down, gt_out, gg_out, gate_out, up_out, down_out, sems):
    copies = [
        pltpu.make_async_copy(gate, gate_out.at[0], sems.at[0]),
        pltpu.make_async_copy(up, up_out.at[0], sems.at[1]),
        pltpu.make_async_copy(down, down_out.at[0], sems.at[2]),
    ]
    for copy in copies:
        copy.start()
    tn = (((0,), (0,)), ((), ()))
    is_x = (iota((256, TOK), 0) % 16) < 8
    picks = pick[...].astype(F32)
    px = jnp.where(is_x, picks, 0.0).astype(BF)
    pd = jnp.where(is_x, 0.0, picks).astype(BF)
    rows = ret[...]
    gt_out[0:FA, :] = lax.dot_general(rows, px, tn, preferred_element_type=F32).astype(BF)
    one = lax.dot_general(rows[0:128], pd[0:128], tn, preferred_element_type=F32)
    two = lax.dot_general(rows[128:256], pd[128:256], tn, preferred_element_type=F32)
    gt_out[FA:F, :] = (one + two)[0:FB].astype(BF)
    gg_out[0:1, :] = one[FB : FB + 1] + one[FB + 1 : FB + 2]
    gg_out[1:2, :] = two[FB : FB + 1] + two[FB + 1 : FB + 2]
    for copy in copies:
        copy.wait()


def per_device(tokens, cotangent, gates, expert_ids, w_gate, w_up, w_down):
    vmem = pl.BlockSpec(memory_space=pltpu.VMEM)
    hbm = pl.BlockSpec(memory_space=pltpu.HBM)
    dma = pltpu.SemaphoreType.DMA
    operands = (tokens.T, cotangent.T, expert_ids.T, gates.T, w_gate, w_up, w_down)
    results = pl.pallas_call(
        comm_kernel,
        out_shape=[
            pltpu.VMEM((256, 256), BF),
            pltpu.VMEM((256, TOK), BF),
            pltpu.VMEM((D, HID), BF),
            pltpu.VMEM((D, HID), BF),
            pltpu.VMEM((HID, D), BF),
        ],
        in_specs=[hbm] * 7,
        out_specs=[vmem] * 5,
        scratch_shapes=[
            pltpu.VMEM((2, TOK), jnp.int32),
            pltpu.VMEM((2, TOK), BF),
            pltpu.VMEM((D, 2 * HID), BF),
            pltpu.VMEM((HID, D), BF),
            pltpu.VMEM((512, 2 * TOK), BF),
            pltpu.VMEM((NDP, 16, 256), BF),
            pltpu.VMEM((NDP, 16, 256), BF),
            pltpu.VMEM((NDP, 16, 256), BF),
            pltpu.VMEM((NDP, 16, 256), BF),
            pltpu.VMEM((D, 256), BF),
            pltpu.VMEM((SLOTS, 2 * HID), F32),
            pltpu.VMEM((HID, SLOTS), F32),
            pltpu.VMEM((2 * HID, SLOTS), BF),
            pltpu.VMEM((HID, SLOTS), BF),
            pltpu.VMEM((8, RB, SLOTS), BF),
            pltpu.VMEM((8, RB, SLOTS), BF),
            pltpu.VMEM((7, RB, SLOTS), BF),
            pltpu.VMEM((7, RB, SLOTS), BF),
            pltpu.VMEM((512, SLOTS), BF),
            pltpu.VMEM((NDP, 16, 256), BF),
            pltpu.VMEM((NDP, 16, 256), BF),
            dma((7,)),
            dma((NDP,)), dma((NDP,)), dma((NDP,)), dma((NDP,)),
            dma((18,)), dma((18,)), dma((20,)), dma((20,)),
            dma((8,)), dma((8,)), dma((7,)), dma((7,)),
            dma((NDP,)), dma((NDP,)),
        ],
        compiler_params=pltpu.CompilerParams(
            collective_id=0, has_side_effects=True, vmem_limit_bytes=40 * 1024 * 1024
        ),
        name="comm",
    )(*(pltpu.with_memory_space_constraint(a, pltpu.HBM) for a in operands))

    gt, gg, gate, up, down = pl.pallas_call(
        finish_kernel,
        out_shape=[
            jax.ShapeDtypeStruct((F, TOK), BF),
            jax.ShapeDtypeStruct((2, TOK), F32),
            jax.ShapeDtypeStruct((1, D, HID), BF),
            jax.ShapeDtypeStruct((1, D, HID), BF),
            jax.ShapeDtypeStruct((1, HID, D), BF),
        ],
        in_specs=[vmem] * 5,
        out_specs=[vmem, vmem, hbm, hbm, hbm],
        scratch_shapes=[dma((3,))],
        compiler_params=pltpu.CompilerParams(vmem_limit_bytes=16 * 1024 * 1024),
        name="finish",
    )(*(pltpu.with_memory_space_constraint(a, pltpu.VMEM) for a in results))
    return gt.T, gg.T, gate, up, down


def solution(mesh):
    in_specs = (
        P("dp", "expert"),
        P("dp", "expert"),
        P("dp", None),
        P("dp", None),
        P("dp", None, "expert"),
        P("dp", None, "expert"),
        P("dp", "expert", None),
    )
    out_specs = (
        P("dp", "expert"),
        P("dp", None),
        P("dp", None, "expert"),
        P("dp", None, "expert"),
        P("dp", "expert", None),
    )
    return jax.shard_map(
        per_device, mesh=mesh, in_specs=in_specs, out_specs=out_specs, check_vma=False
    )
```

```python
import functools

import jax
import jax.numpy as jnp
from jax import lax
from jax.experimental import pallas as pl
from jax.experimental.pallas import tpu as pltpu
from jax.sharding import PartitionSpec as P

MESH = pl.DeviceIdType.MESH
BF = jnp.bfloat16
F32 = jnp.float32

CAP = 8
NDP = 16
NEX = 16
F = 448
FA = 256
FB = F - FA
HB = FB // 2
HA = FA // 2
C = 2 * F
D = NEX * F
HID = 128
TOK = 128
SLOTS = NDP * CAP
NEAR = (0, 2, 14, 4, 12, 6, 10, 1)
FAR = (8, 7, 9, 11, 5, 13, 3, 15)
OFFSETS = NEAR + FAR
FH = F // 2
RB = FH + 16


def iota(shape, dim):
    return lax.broadcasted_iota(jnp.int32, shape, dim)


def split_gate(row):
    hi = row.astype(BF).astype(F32)
    lo = row - hi
    r = iota((16, row.shape[1]), 0)
    return jnp.where(r == 0, hi, jnp.where(r == 1, lo, 0.0)).astype(BF)


def comm_kernel(
    tok_hbm, cot_hbm, ids_hbm, gates_hbm, wg_hbm, wu_hbm, wd_hbm,
    ret_out, pick_out, gate_out, up_out, down_out,
    ids_ref, gates_ref, wgu, wd, ext, sx, rx, al0, al1, pre, back, dd, hg,
    tsend, tsib, rsend, rrecv, rpad, retb, ret,
    w_sem, d_send, d_recv, g_send, g_recv, sib_send, sib_recv,
    ts_send, ts_recv, r_send, r_recv, b_send, b_recv,
):
    me = lax.axis_index("dp")
    j = lax.axis_index("expert")
    y, x, c = j // 8, (j // 2) % 4, j % 2

    def dev(yy, xx, cc):
        return yy * 8 + xx * 2 + cc

    xr, xl, xo = (x + 1) % 4, (x + 3) % 4, (x + 2) % 4
    yo = 1 - y
    sib, xp, xm, yp = dev(y, x, 1 - c), dev(y, xr, c), dev(y, xl, c), dev(yo, x, c)

    started = []

    barrier = pltpu.get_barrier_semaphore()
    for i in FAR + NEAR[:0:-1]:
        pl.semaphore_signal(barrier, inc=1, device_id=((me + i) % NDP, j), device_id_type=MESH)
    chips = [(yy, xx) for yy in (y, yo) for xx in (x, xr, xl, xo)][1:]
    for yy, xx in chips:
        pl.semaphore_signal(barrier, inc=1, device_id=(me, dev(yy, xx, c)), device_id_type=MESH)
    pl.semaphore_signal(barrier, inc=1, device_id=(me, sib), device_id_type=MESH)

    loads = [
        pltpu.make_async_copy(wg_hbm.at[0], wgu.at[:, 0:HID], w_sem.at[0]),
        pltpu.make_async_copy(wu_hbm.at[0], wgu.at[:, HID : 2 * HID], w_sem.at[1]),
        pltpu.make_async_copy(wd_hbm.at[0], wd, w_sem.at[2]),
    ]
    acts = [
        pltpu.make_async_copy(ids_hbm, ids_ref, w_sem.at[5]),
        pltpu.make_async_copy(gates_hbm, gates_ref, w_sem.at[6]),
        pltpu.make_async_copy(tok_hbm, ext.at[0:F, 0:TOK], w_sem.at[3]),
        pltpu.make_async_copy(cot_hbm, ext.at[0:F, TOK : 2 * TOK], w_sem.at[4]),
    ]
    for load in acts + loads:
        load.start()
    acts[0].wait()
    acts[1].wait()

    row = iota((256, TOK), 0)
    ahead = sum(jnp.where(row // 16 == n, o, 0) for n, o in enumerate(OFFSETS))
    expert = (ahead + me) % NDP
    in_first = expert < NDP // 2
    member = jnp.where(in_first, ids_ref[0:1, :], ids_ref[1:2, :]) == expert
    tri = (iota((TOK, TOK), 0) < iota((TOK, TOK), 1)).astype(F32).astype(BF)
    before = jnp.dot(member.astype(F32).astype(BF), tri, preferred_element_type=F32)
    pick = jnp.where(
        jnp.logical_and(member, before == (row % 8).astype(F32)), 1.0, 0.0
    )
    is_x = (row % 16) < 8
    pick_x = jnp.where(is_x, pick, 0.0)
    pick_d = jnp.where(is_x, 0.0, pick)
    pick_out[0] = jnp.where(in_first, pick_x, 0.0).astype(BF)
    pick_out[1] = jnp.where(in_first, 0.0, pick_x).astype(BF)
    pick_out[2] = pick_d.astype(BF)
    gates = gates_ref[...].astype(F32)
    line = iota((512 - F, TOK), 0)
    ext[F:512, 0:TOK] = jnp.where(
        line == 0, gates[0:1, :], jnp.where(line == 1, gates[1:2, :], 0.0)
    ).astype(BF)
    ext[F:512, TOK : 2 * TOK] = jnp.zeros((512 - F, TOK), BF)
    for load in acts[2:]:
        load.wait()
    slots = lax.dot_general(
        jnp.concatenate([pick_x, pick_d], axis=1).astype(BF), ext[...],
        (((1,), (1,)), ((), ())), preferred_element_type=F32,
    ).astype(BF)
    sx[...] = slots.reshape(NDP, 16, 512)
    rx[0] = sx[0]

    r = iota((128, 128), 0)
    k = iota((128, 128), 1)
    perm = jnp.where(k == ((r % 16) // 8) * 64 + (r // 16) * 8 + r % 8, 1.0, 0.0).astype(BF)
    nt = (((1,), (1,)), ((), ()))
    pre[...] = jnp.zeros_like(pre)
    back[...] = jnp.zeros_like(back)

    pl.semaphore_wait(barrier, NDP - 1 + len(chips) + 1)

    d_copies = [None]
    for n, o in enumerate(OFFSETS):
        if o:
            copy = pltpu.make_async_remote_copy(
                src_ref=sx.at[n], dst_ref=rx.at[n],
                send_sem=d_send.at[n], recv_sem=d_recv.at[n],
                device_id=((me + o) % NDP, j), device_id_type=MESH,
            )
            copy.start()
            d_copies.append(copy)
            started.append(copy)

    al = (al0, al1)

    def piece(h, b, lo, n):
        return al[h].at[pl.ds(pl.multiple_of(b * F + lo, 16), n)]

    def move(h, b, lo, n, to, s, sems):
        ref = piece(h, b, lo, n)
        return pltpu.make_async_remote_copy(
            src_ref=ref, dst_ref=ref,
            send_sem=sems[0].at[h, s], recv_sem=sems[1].at[h, s],
            device_id=(me, to), device_id_type=MESH,
        )

    def push(h, b, lo, n, to, s):
        copy = move(h, b, lo, n, to, s, (g_send, g_recv))
        copy.start()
        started.append(copy)

    def share(h, b, lo, n, s):
        copy = move(h, b, lo, n, sib, s, (sib_send, sib_recv))
        copy.start()
        started.append(copy)

    def got(h, b, lo, n, s):
        move(h, b, lo, n, sib, s, (g_send, g_recv)).wait_recv()

    def shared(h, b, lo, n, s):
        move(h, b, lo, n, sib, s, (sib_send, sib_recv)).wait_recv()

    def forward(h, chip):
        at = pl.ds(pl.multiple_of(chip * C, 128), C)
        block = al[h][at, :]
        pre[h] += lax.dot_general(
            block, wgu[at, :], (((0,), (0,)), ((), ())), preferred_element_type=F32
        )
        back[h] += jnp.dot(wd[:, at], block, preferred_element_type=F32)

    gate_rows = [None, None]

    def gather_steps(h):
        b_own, b_xr, b_xl, b_xo = (dev(y, xx, c) for xx in (x, xr, xl, xo))
        o_own, o_xr, o_xl, o_xo = (dev(yo, xx, c) for xx in (x, xr, xl, xo))
        n_own, n_xr, n_xl, n_xo = (dev(y, xx, 1 - c) for xx in (x, xr, xl, xo))
        m_own, m_xr, m_xl, m_xo = (dev(yo, xx, 1 - c) for xx in (x, xr, xl, xo))

        def own():
            for n in range(8 * h, 8 * h + 8):
                if d_copies[n] is not None:
                    d_copies[n].wait_recv()
            turned = lax.dot_general(
                rx[8 * h : 8 * h + 8].reshape(128, 512), perm,
                (((0,), (0,)), ((), ())), preferred_element_type=F32,
            )
            al[h][pl.ds(pl.multiple_of(j * F, 16), F), :] = turned[0:F].astype(BF)
            gate_rows[h] = jnp.where(
                me < NDP // 2, turned[F : F + 1], turned[F + 1 : F + 2]
            )
            push(h, b_own, 0, FA, yp, 0)
            push(h, b_own, 0, FA, xp, 1)
            push(h, b_own, 0, FA, xm, 2)
            push(h, b_own, FA, FB, xp, 4)
            push(h, b_own, FA, FB, xm, 5)
            push(h, b_own, FA, FB, yp, 3)
            share(h, b_own, 0, FA, 0)
            share(h, b_own, FA, FB, 1)

        def first_y():
            got(h, o_own, 0, FA, 0)
            push(h, o_own, 0, FA, xp, 6)
            push(h, o_own, 0, FA, xm, 7)
            share(h, o_own, 0, FA, 2)

        def first_x():
            got(h, b_xl, 0, FA, 1)
            push(h, b_xl, 0, HA, xp, 12)
            share(h, b_xl, 0, FA, 5)
            got(h, b_xr, 0, FA, 2)
            push(h, b_xr, HA, HA, xm, 13)
            share(h, b_xr, 0, FA, 6)

        def second_x():
            got(h, b_xl, FA, FB, 4)
            push(h, b_xl, FA, HB, xp, 8)
            push(h, b_xl, FA, FB, yp, 9)
            share(h, b_xl, FA, FB, 3)
            got(h, b_xr, FA, FB, 5)
            push(h, b_xr, FA + HB, HB, xm, 10)
            push(h, b_xr, FA, FB, yp, 11)
            share(h, b_xr, FA, FB, 4)

        def work_own():
            if h == 0:
                for load in loads:
                    load.wait()
            shared(h, n_own, 0, FA, 0)
            shared(h, n_own, FA, FB, 1)
            forward(h, y * 4 + x)

        def second_y():
            got(h, o_own, FA, FB, 3)
            share(h, o_own, FA, FB, 11)

        def first_yx():
            got(h, o_xl, 0, FA, 6)
            push(h, o_xl, 0, HA, xp, 16)
            share(h, o_xl, 0, FA, 9)
            got(h, o_xr, 0, FA, 7)
            push(h, o_xr, HA, HA, xm, 17)
            share(h, o_xr, 0, FA, 10)

        def work_x():
            shared(h, n_xl, FA, FB, 3)
            shared(h, n_xl, 0, FA, 5)
            forward(h, y * 4 + xl)
            shared(h, n_xr, FA, FB, 4)
            shared(h, n_xr, 0, FA, 6)
            forward(h, y * 4 + xr)

        def second_xx():
            got(h, b_xo, FA, HB, 8)
            push(h, b_xo, FA, HB, yp, 14)
            share(h, b_xo, FA, HB, 7)
            got(h, b_xo, FA + HB, HB, 10)
            push(h, b_xo, FA + HB, HB, yp, 15)
            share(h, b_xo, FA + HB, HB, 8)

        def second_xy():
            got(h, o_xl, FA, FB, 9)
            share(h, o_xl, FA, FB, 12)
            got(h, o_xr, FA, FB, 11)
            share(h, o_xr, FA, FB, 13)

        def work_y():
            shared(h, m_own, 0, FA, 2)
            shared(h, m_own, FA, FB, 11)
            forward(h, yo * 4 + x)

        def first_xx():
            got(h, b_xo, 0, HA, 12)
            share(h, b_xo, 0, HA, 14)
            got(h, b_xo, HA, HA, 13)
            share(h, b_xo, HA, HA, 15)

        def work_xy():
            shared(h, m_xl, 0, FA, 9)
            shared(h, m_xl, FA, FB, 12)
            forward(h, yo * 4 + xl)
            shared(h, m_xr, 0, FA, 10)
            shared(h, m_xr, FA, FB, 13)
            forward(h, yo * 4 + xr)

        def work_xx():
            shared(h, n_xo, FA, HB, 7)
            shared(h, n_xo, FA + HB, HB, 8)
            shared(h, n_xo, 0, HA, 14)
            shared(h, n_xo, HA, HA, 15)
            forward(h, y * 4 + xo)

        def last():
            got(h, o_xo, 0, HA, 16)
            share(h, o_xo, 0, HA, 16)
            got(h, o_xo, HA, HA, 17)
            share(h, o_xo, HA, HA, 17)
            got(h, o_xo, FA, HB, 14)
            share(h, o_xo, FA, HB, 18)
            got(h, o_xo, FA + HB, HB, 15)
            share(h, o_xo, FA + HB, HB, 19)

        def work_last():
            shared(h, m_xo, 0, HA, 16)
            shared(h, m_xo, HA, HA, 17)
            shared(h, m_xo, FA, HB, 18)
            shared(h, m_xo, FA + HB, HB, 19)
            forward(h, yo * 4 + xo)

        return [
            (0.0, own), (3.9, first_y), (4.0, first_x), (5.0, second_x), (6.0, work_own),
            (7.5, second_y), (8.0, first_yx), (8.6, work_x), (9.0, second_xx), (9.3, second_xy),
            (9.4, work_y), (9.9, first_xx), (10.5, work_xy), (11.2, work_xx), (11.9, last),
            (13.0, work_last),
        ]

    gate_terms = [None, None]

    def units(h):
        turned_pre = pre[h].T
        pg, pu = turned_pre[0:HID], turned_pre[HID : 2 * HID]
        sig = jax.nn.sigmoid(pg)
        act = pg * sig
        hidden = act * pu
        bk = pltpu.roll(back[h], 64, 1)
        ok = iota((HID, 128), 1) < 64
        gate_terms[h] = split_gate(
            jnp.sum(
                jnp.where(ok, bk * hidden.astype(BF).astype(F32), 0.0), axis=0, keepdims=True
            )
        )
        dhid = gate_rows[h] * bk
        dg = jnp.where(ok, dhid * pu * sig * (1.0 + pg * (1.0 - sig)), 0.0)
        du = jnp.where(ok, dhid * act, 0.0)
        dd[h, 0:HID, :] = dg.astype(BF)
        dd[h, HID : 2 * HID, :] = du.astype(BF)
        dd[h, 2 * HID : 3 * HID, :] = pltpu.roll(dg, 64, 1).astype(BF)
        dd[h, 3 * HID : 4 * HID, :] = pltpu.roll(du, 64, 1).astype(BF)
        hg[h] = pltpu.roll(jnp.where(ok, hidden * gate_rows[h], 0.0), 64, 1).astype(BF)

    def term(h, b):
        lo = wgu[pl.ds(pl.multiple_of(b * F, 16), FH), :]
        hi = wgu[pl.ds(pl.multiple_of(b * F + FH, 16), FH), :]
        return jnp.dot(lo, dd[h, 0 : 2 * HID, :], preferred_element_type=F32) + jnp.dot(
            hi, dd[h, 2 * HID : 4 * HID, :], preferred_element_type=F32
        )

    def gate_total(*blocks):
        total = sum(block.astype(F32) for block in blocks)
        return jnp.sum(total, axis=0, keepdims=True)

    order = [(yo, xo), (yo, xl), (yo, xr), (y, xo), (yo, x), (y, xl), (y, xr), (y, x)]
    ts_copies = ([], [])
    r_copies = ([], [])
    mine = [None, None]

    def to_sibling(h):
        for n, (yy, xx) in enumerate(order):
            tsend[h, n, 0:FH, :] = term(h, dev(yy, xx, 1 - c)).astype(BF)
            tsend[h, n, FH:RB, :] = gate_terms[h]
            copy = pltpu.make_async_remote_copy(
                src_ref=tsend.at[h, n], dst_ref=tsib.at[h, n],
                send_sem=ts_send.at[h, n], recv_sem=ts_recv.at[h, n],
                device_id=(me, sib), device_id_type=MESH,
            )
            copy.start()
            ts_copies[h].append(copy)
            started.append(copy)

    def to_chips(h):
        for n, (yy, xx) in enumerate(order):
            part = term(h, dev(yy, xx, c))
            ts_copies[h][n].wait_recv()
            part = part + tsib[h, n, 0:FH, :].astype(F32)
            gate_part = gate_total(gate_terms[h], tsib[h, n, FH:RB, :])
            if n < 7:
                rsend[h, n, 0:FH, :] = part.astype(BF)
                rsend[h, n, FH:RB, :] = split_gate(gate_part)
                copy = pltpu.make_async_remote_copy(
                    src_ref=rsend.at[h, n], dst_ref=rrecv.at[h, n],
                    send_sem=r_send.at[h, n], recv_sem=r_recv.at[h, n],
                    device_id=(me, dev(yy, xx, c)), device_id_type=MESH,
                )
                copy.start()
                r_copies[h].append(copy)
                started.append(copy)
            else:
                mine[h] = (part, gate_part)

    b_copies = [None]

    def give_back(h):
        total, gate_sum = mine[h]
        for n in range(6, -1, -1):
            r_copies[h][n].wait_recv()
            total = total + rrecv[h, n, 0:FH, :].astype(F32)
            gate_sum = gate_sum + gate_total(rrecv[h, n, FH:RB, :])
        rpad[0:FH, :] = total.astype(BF)
        rpad[FH:RB, :] = split_gate(gate_sum)
        rpad[RB:256, :] = jnp.zeros((256 - RB, 128), BF)
        rows = lax.dot_general(perm, rpad[...], nt, preferred_element_type=F32)
        retb[8 * h : 8 * h + 8] = rows.astype(BF).reshape(8, 16, 256)
        for n in range(8 * h, 8 * h + 8):
            o = OFFSETS[n]
            if o:
                copy = pltpu.make_async_remote_copy(
                    src_ref=retb.at[n], dst_ref=ret.at[n],
                    send_sem=b_send.at[n], recv_sem=b_recv.at[n],
                    device_id=((me + NDP - o) % NDP, j), device_id_type=MESH,
                )
                copy.start()
                b_copies.append(copy)
                started.append(copy)
            else:
                ret[0] = retb[0]

    def grads(i, carry):
        at = pl.ds(pl.multiple_of(i * C, 128), C)
        near, far = al0[at, :], al1[at, :]
        both = lax.dot_general(near, dd[0, 0 : 2 * HID, :], nt, preferred_element_type=F32)
        both += lax.dot_general(far, dd[1, 0 : 2 * HID, :], nt, preferred_element_type=F32)
        gate_out[at, :] = both[:, 0:HID].astype(BF)
        up_out[at, :] = both[:, HID : 2 * HID].astype(BF)
        down = lax.dot_general(hg[0], near, nt, preferred_element_type=F32)
        down += lax.dot_general(hg[1], far, nt, preferred_element_type=F32)
        down_out[:, at] = down.astype(BF)
        return carry

    steps = [(1.2 * t, step) for t, step in gather_steps(0)]
    steps += [(2.5 + 1.05 * t, step) for t, step in gather_steps(1)]
    steps += [
        (16.35, functools.partial(units, 1)),
        (16.45, functools.partial(to_sibling, 1)),
        (17.85, functools.partial(to_chips, 1)),
        (17.96, functools.partial(units, 0)),
        (17.97, functools.partial(to_sibling, 0)),
        (17.98, functools.partial(to_chips, 0)),
        (20.0, lambda: lax.fori_loop(0, 2, grads, 0)),
        (21.0, functools.partial(give_back, 1)),
        (22.0, lambda: lax.fori_loop(2, D // C, grads, 0)),
        (24.0, functools.partial(give_back, 0)),
    ]
    for _, step in sorted(steps, key=lambda pair: pair[0]):
        step()

    for copy in b_copies[1:]:
        copy.wait_recv()
    ret_out[...] = ret[...].reshape(256, 256)
    for copy in started:
        copy.wait_send()


def finish_kernel(ret, pick, gate, up, down, gt_out, gg_out, gate_out, up_out, down_out, sems):
    copies = [
        pltpu.make_async_copy(gate, gate_out.at[0], sems.at[0]),
        pltpu.make_async_copy(up, up_out.at[0], sems.at[1]),
        pltpu.make_async_copy(down, down_out.at[0], sems.at[2]),
    ]
    for copy in copies:
        copy.start()
    tn = (((0,), (0,)), ((), ()))
    rows = ret[...]
    one, two, low = (
        lax.dot_general(rows, pick[n], tn, preferred_element_type=F32) for n in range(3)
    )
    gt_out[0:FH, :] = (one + two)[0:FH].astype(BF)
    gt_out[FH:F, :] = low[0:FH].astype(BF)
    gg_out[0:1, :] = one[FH : FH + 1] + one[FH + 1 : FH + 2]
    gg_out[1:2, :] = two[FH : FH + 1] + two[FH + 1 : FH + 2]
    for copy in copies:
        copy.wait()


def per_device(tokens, cotangent, gates, expert_ids, w_gate, w_up, w_down):
    vmem = pl.BlockSpec(memory_space=pltpu.VMEM)
    hbm = pl.BlockSpec(memory_space=pltpu.HBM)
    dma = pltpu.SemaphoreType.DMA
    operands = (tokens.T, cotangent.T, expert_ids.T, gates.T, w_gate, w_up, w_down)
    results = pl.pallas_call(
        comm_kernel,
        out_shape=[
            pltpu.VMEM((256, 256), BF),
            pltpu.VMEM((3, 256, TOK), BF),
            pltpu.VMEM((D, HID), BF),
            pltpu.VMEM((D, HID), BF),
            pltpu.VMEM((HID, D), BF),
        ],
        in_specs=[hbm] * 7,
        out_specs=[vmem] * 5,
        scratch_shapes=[
            pltpu.VMEM((2, TOK), jnp.int32),
            pltpu.VMEM((2, TOK), BF),
            pltpu.VMEM((D, 2 * HID), BF),
            pltpu.VMEM((HID, D), BF),
            pltpu.VMEM((512, 2 * TOK), BF),
            pltpu.VMEM((NDP, 16, 512), BF),
            pltpu.VMEM((NDP, 16, 512), BF),
            pltpu.VMEM((D, 128), BF),
            pltpu.VMEM((D, 128), BF),
            pltpu.VMEM((2, 128, 2 * HID), F32),
            pltpu.VMEM((2, HID, 128), F32),
            pltpu.VMEM((2, 4 * HID, 128), BF),
            pltpu.VMEM((2, HID, 128), BF),
            pltpu.VMEM((2, 8, RB, 128), BF),
            pltpu.VMEM((2, 8, RB, 128), BF),
            pltpu.VMEM((2, 7, RB, 128), BF),
            pltpu.VMEM((2, 7, RB, 128), BF),
            pltpu.VMEM((256, 128), BF),
            pltpu.VMEM((NDP, 16, 256), BF),
            pltpu.VMEM((NDP, 16, 256), BF),
            dma((7,)),
            dma((NDP,)), dma((NDP,)),
            dma((2, 18)), dma((2, 18)), dma((2, 20)), dma((2, 20)),
            dma((2, 8)), dma((2, 8)), dma((2, 7)), dma((2, 7)),
            dma((NDP,)), dma((NDP,)),
        ],
        compiler_params=pltpu.CompilerParams(
            collective_id=0, has_side_effects=True, vmem_limit_bytes=40 * 1024 * 1024
        ),
        name="comm",
    )(*(pltpu.with_memory_space_constraint(a, pltpu.HBM) for a in operands))

    gt, gg, gate, up, down = pl.pallas_call(
        finish_kernel,
        out_shape=[
            jax.ShapeDtypeStruct((F, TOK), BF),
            jax.ShapeDtypeStruct((2, TOK), F32),
            jax.ShapeDtypeStruct((1, D, HID), BF),
            jax.ShapeDtypeStruct((1, D, HID), BF),
            jax.ShapeDtypeStruct((1, HID, D), BF),
        ],
        in_specs=[vmem] * 5,
        out_specs=[vmem, vmem, hbm, hbm, hbm],
        scratch_shapes=[dma((3,))],
        compiler_params=pltpu.CompilerParams(vmem_limit_bytes=16 * 1024 * 1024),
        name="finish",
    )(*(pltpu.with_memory_space_constraint(a, pltpu.VMEM) for a in results))
    return gt.T, gg.T, gate, up, down


def solution(mesh):
    in_specs = (
        P("dp", "expert"),
        P("dp", "expert"),
        P("dp", None),
        P("dp", None),
        P("dp", None, "expert"),
        P("dp", None, "expert"),
        P("dp", "expert", None),
    )
    out_specs = (
        P("dp", "expert"),
        P("dp", None),
        P("dp", None, "expert"),
        P("dp", None, "expert"),
        P("dp", "expert", None),
    )
    return jax.shard_map(
        per_device, mesh=mesh, in_specs=in_specs, out_specs=out_specs, check_vma=False
    )
```

```python
import functools

import jax
import jax.numpy as jnp
from jax import lax
from jax.experimental import pallas as pl
from jax.experimental.pallas import tpu as pltpu
from jax.sharding import PartitionSpec as P

MESH = pl.DeviceIdType.MESH
BF = jnp.bfloat16
F32 = jnp.float32

CAP = 8
NDP = 16
NEX = 16
F = 448
FA = 256
FB = F - FA
HB = FB // 2
HA = FA // 2
C = 2 * F
D = NEX * F
HID = 128
TOK = 128
SLOTS = NDP * CAP
NEAR = (0, 2, 14, 4, 12, 6, 10, 1)
FAR = (8, 7, 9, 11, 5, 13, 3, 15)
OFFSETS = NEAR + FAR
FH = F // 2
YR = 144
RB = FH + 16

ORDER = (
    "0own 0Wown 1own 0Aoo", "0Bxl 0Bxr 0Axl 0Axr", "0Boo 1Wown 0Wxl 0Wxr",
    "1Bxl 1Bxr 1Aoo 0Woo", "1Axl 1Axr 1Boo 0Boxl", "1Wxl 1Wxr 1Woo 0Bxo1",
    "0Bxo2 0Aoxl 0Aoxr 0Boxr", "0Axo1 0Axo2 1Bxo1 1Bxo2", "1Boxl 0Woxl 0Woxr 1Boxr",
    "0Wxo 1Aoxl 1Aoxr 0Boxo1", "1Axo1 1Axo2 0Boxo2 1Boxo1", "0Aoxo1 0Aoxo2 1Woxl 1Boxo2",
    "1Woxr 1Wxo 0Woxo 1Aoxo1", "1Aoxo2 0U 1Woxo 1U", "0T0 0T1 0T2 0T3",
    "0T4 0T5 0T6 0T7", "0C0 0C1 0C2 0C3", "0C4 0C5 0C6 0C7",
    "0N0 0N1 0N2 0N3", "0N4 0N5 0N6 0N7", "1P2xo 1P2xr 1P2xl 1Q2",
    "0P2xo 0P2xr 0P2xl 0Q2", "0G02 1B 0B 0G28",
)


def iota(shape, dim):
    return lax.broadcasted_iota(jnp.int32, shape, dim)


def split_gate(row):
    hi = row.astype(BF).astype(F32)
    lo = row - hi
    r = iota((16, row.shape[1]), 0)
    return jnp.where(r == 0, hi, jnp.where(r == 1, lo, 0.0)).astype(BF)


def comm_kernel(
    tok_hbm, cot_hbm, ids_hbm, gates_hbm, wg_hbm, wu_hbm, wd_hbm,
    ret_out, pick_out, gate_out, up_out, down_out,
    ids_ref, gates_ref, wgu, wt, ext, sx, rx, al0, al1, acc, dd, hg,
    tsend, tsib, y_keep, y_send, y_recv, yx_send, yx_recv, x_keep, x_send, x_recv, xy_send, xy_recv,
    rpad, retb, ret,
    w_sem, d_send, d_recv, g_send, g_recv, sib_send, sib_recv,
    ts_send, ts_recv, ys_sem, yr_sem, yxs_sem, yxr_sem, xs_sem, xr_sem, xys_sem, xyr_sem,
    b_send, b_recv,
):
    me = lax.axis_index("dp")
    j = lax.axis_index("expert")
    y, x, c = j // 8, (j // 2) % 4, j % 2

    def dev(yy, xx, cc):
        return yy * 8 + xx * 2 + cc

    xr, xl, xo = (x + 1) % 4, (x + 3) % 4, (x + 2) % 4
    yo = 1 - y
    sib, xp, xm, yp = dev(y, x, 1 - c), dev(y, xr, c), dev(y, xl, c), dev(yo, x, c)

    started = []

    barrier = pltpu.get_barrier_semaphore()
    for i in FAR + NEAR[:0:-1]:
        pl.semaphore_signal(barrier, inc=1, device_id=((me + i) % NDP, j), device_id_type=MESH)
    chips = [(y, xr), (y, xl), (y, xo), (yo, x)]
    for yy, xx in chips:
        pl.semaphore_signal(barrier, inc=1, device_id=(me, dev(yy, xx, c)), device_id_type=MESH)
    pl.semaphore_signal(barrier, inc=1, device_id=(me, sib), device_id_type=MESH)

    loads = [
        pltpu.make_async_copy(wg_hbm.at[0], wgu.at[:, 0:HID], w_sem.at[0]),
        pltpu.make_async_copy(wu_hbm.at[0], wgu.at[:, HID : 2 * HID], w_sem.at[1]),
        pltpu.make_async_copy(wd_hbm.at[0], wt.at[2 * HID : 3 * HID, :], w_sem.at[2]),
    ]
    acts = [
        pltpu.make_async_copy(ids_hbm, ids_ref, w_sem.at[5]),
        pltpu.make_async_copy(gates_hbm, gates_ref, w_sem.at[6]),
        pltpu.make_async_copy(tok_hbm, ext.at[0:F, 0:TOK], w_sem.at[3]),
        pltpu.make_async_copy(cot_hbm, ext.at[0:F, TOK : 2 * TOK], w_sem.at[4]),
    ]
    for load in acts + loads:
        load.start()
    acts[0].wait()
    acts[1].wait()

    row = iota((256, TOK), 0)
    ahead = sum(jnp.where(row // 16 == n, o, 0) for n, o in enumerate(OFFSETS))
    expert = (ahead + me) % NDP
    in_first = expert < NDP // 2
    member = jnp.where(in_first, ids_ref[0:1, :], ids_ref[1:2, :]) == expert
    tri = (iota((TOK, TOK), 0) < iota((TOK, TOK), 1)).astype(F32).astype(BF)
    before = jnp.dot(member.astype(F32).astype(BF), tri, preferred_element_type=F32)
    pick = jnp.where(
        jnp.logical_and(member, before == (row % 8).astype(F32)), 1.0, 0.0
    )
    is_x = (row % 16) < 8
    pick_x = jnp.where(is_x, pick, 0.0)
    pick_d = jnp.where(is_x, 0.0, pick)
    pick_out[0] = jnp.where(in_first, pick_x, 0.0).astype(BF)
    pick_out[1] = jnp.where(in_first, 0.0, pick_x).astype(BF)
    pick_out[2] = pick_d.astype(BF)
    gates = gates_ref[...].astype(F32)
    line = iota((512 - F, TOK), 0)
    ext[F:512, 0:TOK] = jnp.where(
        line == 0, gates[0:1, :], jnp.where(line == 1, gates[1:2, :], 0.0)
    ).astype(BF)
    ext[F:512, TOK : 2 * TOK] = jnp.zeros((512 - F, TOK), BF)
    for load in acts[2:]:
        load.wait()
    slots = lax.dot_general(
        jnp.concatenate([pick_x, pick_d], axis=1).astype(BF), ext[...],
        (((1,), (1,)), ((), ())), preferred_element_type=F32,
    ).astype(BF)
    sx[...] = slots.reshape(NDP, 16, 512)
    rx[0] = sx[0]

    r = iota((128, 128), 0)
    k = iota((128, 128), 1)
    perm = jnp.where(k == ((r % 16) // 8) * 64 + (r // 16) * 8 + r % 8, 1.0, 0.0).astype(BF)
    nt = (((1,), (1,)), ((), ()))
    acc[...] = jnp.zeros_like(acc)

    pl.semaphore_wait(barrier, NDP - 1 + len(chips) + 1)

    d_copies = [None]
    for n, o in enumerate(OFFSETS):
        if o:
            copy = pltpu.make_async_remote_copy(
                src_ref=sx.at[n], dst_ref=rx.at[n],
                send_sem=d_send.at[n], recv_sem=d_recv.at[n],
                device_id=((me + o) % NDP, j), device_id_type=MESH,
            )
            copy.start()
            d_copies.append(copy)
            started.append(copy)

    for load in loads:
        load.wait()

    def turn(i, carry):
        at = pl.ds(pl.multiple_of(i * C, 128), C)
        wt[0 : 2 * HID, at] = wgu[at, :].T
        return carry

    lax.fori_loop(0, D // C, turn, 0)

    al = (al0, al1)

    def piece(h, b, lo, n):
        return al[h].at[pl.ds(pl.multiple_of(b * F + lo, 16), n)]

    def move(h, b, lo, n, to, s, sems):
        ref = piece(h, b, lo, n)
        return pltpu.make_async_remote_copy(
            src_ref=ref, dst_ref=ref,
            send_sem=sems[0].at[h, s], recv_sem=sems[1].at[h, s],
            device_id=(me, to), device_id_type=MESH,
        )

    def push(h, b, lo, n, to, s):
        copy = move(h, b, lo, n, to, s, (g_send, g_recv))
        copy.start()
        started.append(copy)

    def share(h, b, lo, n, s):
        copy = move(h, b, lo, n, sib, s, (sib_send, sib_recv))
        copy.start()
        started.append(copy)

    def got(h, b, lo, n, s):
        move(h, b, lo, n, sib, s, (g_send, g_recv)).wait_recv()

    def shared(h, b, lo, n, s):
        move(h, b, lo, n, sib, s, (sib_send, sib_recv)).wait_recv()

    def forward(h, chip):
        at = pl.ds(pl.multiple_of(chip * C, 128), C)
        acc[h] += jnp.dot(wt[:, at], al[h][at, :], preferred_element_type=F32)

    gate_rows = [None, None]

    def own(h):
        for n in range(8 * h, 8 * h + 8):
            if d_copies[n] is not None:
                d_copies[n].wait_recv()
        turned = lax.dot_general(
            rx[8 * h : 8 * h + 8].reshape(128, 512), perm,
            (((0,), (0,)), ((), ())), preferred_element_type=F32,
        )
        al[h][pl.ds(pl.multiple_of(j * F, 16), F), :] = turned[0:F].astype(BF)
        gate_rows[h] = jnp.where(me < NDP // 2, turned[F : F + 1], turned[F + 1 : F + 2])
        push(h, j, FA, FB, xp, 4)
        push(h, j, FA, FB, xm, 5)
        push(h, j, 0, FA, yp, 0)
        push(h, j, 0, FA, xp, 1)
        push(h, j, 0, FA, xm, 2)
        push(h, j, FA, FB, yp, 3)
        share(h, j, 0, FA, 0)
        share(h, j, FA, FB, 1)

    arrivals = {
        "Aoo": ((yo, x), 0, FA, 0, 2, ((0, FA, xp, 6), (0, FA, xm, 7))),
        "Axl": ((y, xl), 0, FA, 1, 5, ((0, HA, xp, 12),)),
        "Axr": ((y, xr), 0, FA, 2, 6, ((HA, HA, xm, 13),)),
        "Boo": ((yo, x), FA, FB, 3, 11, ()),
        "Bxl": ((y, xl), FA, FB, 4, 3, ((FA, HB, xp, 8), (FA, FB, yp, 9))),
        "Bxr": ((y, xr), FA, FB, 5, 4, ((FA + HB, HB, xm, 10), (FA, FB, yp, 11))),
        "Aoxl": ((yo, xl), 0, FA, 6, 9, ((0, HA, xp, 16),)),
        "Aoxr": ((yo, xr), 0, FA, 7, 10, ((HA, HA, xm, 17),)),
        "Bxo1": ((y, xo), FA, HB, 8, 7, ((FA, HB, yp, 14),)),
        "Bxo2": ((y, xo), FA + HB, HB, 10, 8, ((FA + HB, HB, yp, 15),)),
        "Boxl": ((yo, xl), FA, FB, 9, 12, ()),
        "Boxr": ((yo, xr), FA, FB, 11, 13, ()),
        "Axo1": ((y, xo), 0, HA, 12, 14, ()),
        "Axo2": ((y, xo), HA, HA, 13, 15, ()),
        "Boxo1": ((yo, xo), FA, HB, 14, 18, ()),
        "Boxo2": ((yo, xo), FA + HB, HB, 15, 19, ()),
        "Aoxo1": ((yo, xo), 0, HA, 16, 16, ()),
        "Aoxo2": ((yo, xo), HA, HA, 17, 17, ()),
    }
    works = {
        "Wown": ((y, x), ((0, FA, 0), (FA, FB, 1))),
        "Wxl": ((y, xl), ((FA, FB, 3), (0, FA, 5))),
        "Wxr": ((y, xr), ((FA, FB, 4), (0, FA, 6))),
        "Woo": ((yo, x), ((0, FA, 2), (FA, FB, 11))),
        "Woxl": ((yo, xl), ((0, FA, 9), (FA, FB, 12))),
        "Woxr": ((yo, xr), ((0, FA, 10), (FA, FB, 13))),
        "Wxo": ((y, xo), ((FA, HB, 7), (FA + HB, HB, 8), (0, HA, 14), (HA, HA, 15))),
        "Woxo": ((yo, xo), ((0, HA, 16), (HA, HA, 17), (FA, HB, 18), (FA + HB, HB, 19))),
    }

    def arrive(h, name):
        (yy, xx), lo, n, s, to_sib, onward = arrivals[name]
        b = dev(yy, xx, c)
        got(h, b, lo, n, s)
        for first, count, to, sem in onward:
            push(h, b, first, count, to, sem)
        share(h, b, lo, n, to_sib)

    def work(h, name):
        (yy, xx), parts = works[name]
        for lo, n, s in parts:
            shared(h, dev(yy, xx, 1 - c), lo, n, s)
        forward(h, yy * 4 + xx)

    gate_terms = [None, None]

    def units(h):
        pg, pu = acc[h, 0:HID, :], acc[h, HID : 2 * HID, :]
        sig = jax.nn.sigmoid(pg)
        act = pg * sig
        hidden = act * pu
        bk = pltpu.roll(acc[h, 2 * HID : 3 * HID, :], 64, 1)
        ok = iota((HID, 128), 1) < 64
        gate_terms[h] = split_gate(
            jnp.sum(
                jnp.where(ok, bk * hidden.astype(BF).astype(F32), 0.0), axis=0, keepdims=True
            )
        )
        dhid = gate_rows[h] * bk
        dg = jnp.where(ok, dhid * pu * sig * (1.0 + pg * (1.0 - sig)), 0.0)
        du = jnp.where(ok, dhid * act, 0.0)
        lanes = slice(128 * h, 128 * h + 128)
        dd[0:HID, lanes] = dg.astype(BF)
        dd[HID : 2 * HID, lanes] = du.astype(BF)
        dd[2 * HID : 3 * HID, lanes] = pltpu.roll(dg, 64, 1).astype(BF)
        dd[3 * HID : 4 * HID, lanes] = pltpu.roll(du, 64, 1).astype(BF)
        hg[h] = pltpu.roll(jnp.where(ok, hidden * gate_rows[h], 0.0), 64, 1).astype(BF)

    def term(b):
        lo = wgu[pl.ds(pl.multiple_of(b * F, 16), FH), :]
        hi = wgu[pl.ds(pl.multiple_of(b * F + FH, 16), FH), :]
        return jnp.dot(lo, dd[0 : 2 * HID, :], preferred_element_type=F32) + jnp.dot(
            hi, dd[2 * HID : 4 * HID, :], preferred_element_type=F32
        )

    def gate_total(*blocks):
        total = sum(block.astype(F32) for block in blocks)
        return jnp.sum(total, axis=0, keepdims=True)

    columns = (xo, xr, xl, x)
    ts_copies, y_copies, yx_copies, x_copies, xy_copies = {}, {}, {}, {}, {}

    def send(copies, key, src, dst, send_sem, recv_sem, to):
        copy = pltpu.make_async_remote_copy(
            src_ref=src, dst_ref=dst, send_sem=send_sem, recv_sem=recv_sem,
            device_id=(me, to), device_id_type=MESH,
        )
        copy.start()
        copies[key] = copy
        started.append(copy)

    def to_sibling(n):
        tsend[n, 0:FH, :] = term(dev((yo, y)[n % 2], columns[n // 2], 1 - c)).astype(BF)
        tsend[n, FH:RB, 0:128] = gate_terms[0]
        tsend[n, FH:RB, 128:256] = gate_terms[1]
        send(ts_copies, n, tsend.at[n], tsib.at[n], ts_send.at[n], ts_recv.at[n], sib)

    def to_chips(n):
        col, mine = n // 2, n % 2
        both = term(dev((yo, y)[mine], columns[col], c))
        ts_copies[n].wait_recv()
        both = both + tsib[n, 0:FH, :].astype(F32)
        for h in (1, 0):
            lanes = slice(128 * h, 128 * h + 128)
            part = both[:, lanes]
            gate_part = gate_total(gate_terms[h], tsib[n, FH:RB, lanes])
            if mine:
                y_keep[h, col] = part[0:YR]
            else:
                y_send[h, col] = part[0:YR].astype(BF)
            if col == 3:
                x_keep[h, mine, 0 : FH - YR, :] = part[YR:FH]
                x_keep[h, mine, FH - YR :, :] = jnp.where(
                    iota((16, 128), 0) == 0, gate_part, 0.0
                )
            else:
                x_send[h, col, mine, 0 : FH - YR, :] = part[YR:FH].astype(BF)
                x_send[h, col, mine, FH - YR :, :] = split_gate(gate_part)
            if h == 1:
                leave(h, n)

    def leave(h, n):
        col, mine = n // 2, n % 2
        if not mine:
            send(
                y_copies, (h, col), y_send.at[h, col], y_recv.at[h, col],
                ys_sem.at[h, col], yr_sem.at[h, col], yp,
            )
        elif col < 3:
            send(
                x_copies, (h, col), x_send.at[h, col], x_recv.at[h, col],
                xs_sem.at[h, col], xr_sem.at[h, col], dev(y, columns[col], c),
            )

    def then_x(h, col):
        y_copies[h, col].wait_recv()
        yx_send[h, col] = (y_keep[h, col] + y_recv[h, col].astype(F32)).astype(BF)
        send(
            yx_copies, (h, col), yx_send.at[h, col], yx_recv.at[h, col],
            yxs_sem.at[h, col], yxr_sem.at[h, col], dev(y, columns[col], c),
        )

    def x_total(h, mine):
        total = x_keep[h, mine]
        for col in range(3):
            total = total + x_recv[h, col, mine].astype(F32)
        return total

    def then_y(h):
        for col in range(3):
            x_copies[h, col].wait_recv()
        total = x_total(h, 0)
        xy_send[h, 0 : FH - YR, :] = total[0 : FH - YR].astype(BF)
        xy_send[h, FH - YR :, :] = split_gate(gate_total(total[FH - YR :]))
        send(xy_copies, h, xy_send.at[h], xy_recv.at[h], xys_sem.at[h], xyr_sem.at[h], yp)

    b_copies = []

    def give_back(h):
        second = x_total(h, 1)
        y_copies[h, 3].wait_recv()
        first = y_keep[h, 3] + y_recv[h, 3].astype(F32)
        for col in range(3):
            yx_copies[h, col].wait_recv()
            first = first + yx_recv[h, col].astype(F32)
        xy_copies[h].wait_recv()
        second = second + xy_recv[h].astype(F32)
        rpad[0:YR, :] = first.astype(BF)
        rpad[YR:FH, :] = second[0 : FH - YR].astype(BF)
        rpad[FH:RB, :] = split_gate(gate_total(second[FH - YR :]))
        rpad[RB:256, :] = jnp.zeros((256 - RB, 128), BF)
        rows = lax.dot_general(perm, rpad[...], nt, preferred_element_type=F32)
        retb[8 * h : 8 * h + 8] = rows.astype(BF).reshape(8, 16, 256)
        for n in range(8 * h, 8 * h + 8):
            o = OFFSETS[n]
            if o:
                copy = pltpu.make_async_remote_copy(
                    src_ref=retb.at[n], dst_ref=ret.at[n],
                    send_sem=b_send.at[n], recv_sem=b_recv.at[n],
                    device_id=((me + NDP - o) % NDP, j), device_id_type=MESH,
                )
                copy.start()
                b_copies.append(copy)
                started.append(copy)
            else:
                ret[0] = retb[0]

    def grads(i, carry):
        at = pl.ds(pl.multiple_of(i * C, 128), C)
        near, far = al0[at, :], al1[at, :]
        both = lax.dot_general(near, dd[0 : 2 * HID, 0:128], nt, preferred_element_type=F32)
        both += lax.dot_general(far, dd[0 : 2 * HID, 128:256], nt, preferred_element_type=F32)
        gate_out[at, :] = both[:, 0:HID].astype(BF)
        up_out[at, :] = both[:, HID : 2 * HID].astype(BF)
        down = lax.dot_general(hg[0], near, nt, preferred_element_type=F32)
        down += lax.dot_general(hg[1], far, nt, preferred_element_type=F32)
        down_out[:, at] = down.astype(BF)
        return carry

    for name in " ".join(ORDER).split():
        h, name = int(name[0]), name[1:]
        if name == "own":
            own(h)
        elif name in arrivals:
            arrive(h, name)
        elif name in works:
            work(h, name)
        elif name == "U":
            units(h)
        elif name[0] == "T":
            to_sibling(int(name[1:]))
        elif name[0] == "C":
            to_chips(int(name[1:]))
        elif name[0] == "N":
            leave(h, int(name[1:]))
        elif name == "Q2":
            then_y(h)
        elif name[:2] == "P2":
            then_x(h, ("xo", "xr", "xl").index(name[2:]))
        elif name == "B":
            give_back(h)
        elif name[0] == "G":
            lax.fori_loop(int(name[1]), int(name[2]), grads, 0)

    for copy in b_copies:
        copy.wait_recv()
    ret_out[...] = ret[...].reshape(256, 256)
    for copy in started:
        copy.wait_send()


def finish_kernel(ret, pick, gate, up, down, gt_out, gg_out, gate_out, up_out, down_out, sems):
    copies = [
        pltpu.make_async_copy(gate, gate_out.at[0], sems.at[0]),
        pltpu.make_async_copy(up, up_out.at[0], sems.at[1]),
        pltpu.make_async_copy(down, down_out.at[0], sems.at[2]),
    ]
    for copy in copies:
        copy.start()
    tn = (((0,), (0,)), ((), ()))
    rows = ret[...]
    one, two, low = (
        lax.dot_general(rows, pick[n], tn, preferred_element_type=F32) for n in range(3)
    )
    gt_out[0:FH, :] = (one + two)[0:FH].astype(BF)
    gt_out[FH:F, :] = low[0:FH].astype(BF)
    gg_out[0:1, :] = one[FH : FH + 1] + one[FH + 1 : FH + 2]
    gg_out[1:2, :] = two[FH : FH + 1] + two[FH + 1 : FH + 2]
    for copy in copies:
        copy.wait()


def per_device(tokens, cotangent, gates, expert_ids, w_gate, w_up, w_down):
    vmem = pl.BlockSpec(memory_space=pltpu.VMEM)
    hbm = pl.BlockSpec(memory_space=pltpu.HBM)
    dma = pltpu.SemaphoreType.DMA
    operands = (tokens.T, cotangent.T, expert_ids.T, gates.T, w_gate, w_up, w_down)
    results = pl.pallas_call(
        comm_kernel,
        out_shape=[
            pltpu.VMEM((256, 256), BF),
            pltpu.VMEM((3, 256, TOK), BF),
            pltpu.VMEM((D, HID), BF),
            pltpu.VMEM((D, HID), BF),
            pltpu.VMEM((HID, D), BF),
        ],
        in_specs=[hbm] * 7,
        out_specs=[vmem] * 5,
        scratch_shapes=[
            pltpu.VMEM((2, TOK), jnp.int32),
            pltpu.VMEM((2, TOK), BF),
            pltpu.VMEM((D, 2 * HID), BF),
            pltpu.VMEM((3 * HID, D), BF),
            pltpu.VMEM((512, 2 * TOK), BF),
            pltpu.VMEM((NDP, 16, 512), BF),
            pltpu.VMEM((NDP, 16, 512), BF),
            pltpu.VMEM((D, 128), BF),
            pltpu.VMEM((D, 128), BF),
            pltpu.VMEM((2, 3 * HID, 128), F32),
            pltpu.VMEM((4 * HID, 256), BF),
            pltpu.VMEM((2, HID, 128), BF),
            pltpu.VMEM((8, RB, 256), BF),
            pltpu.VMEM((8, RB, 256), BF),
            pltpu.VMEM((2, 4, YR, 128), F32),
            pltpu.VMEM((2, 4, YR, 128), BF),
            pltpu.VMEM((2, 4, YR, 128), BF),
            pltpu.VMEM((2, 3, YR, 128), BF),
            pltpu.VMEM((2, 3, YR, 128), BF),
            pltpu.VMEM((2, 2, RB - YR, 128), F32),
            pltpu.VMEM((2, 3, 2, RB - YR, 128), BF),
            pltpu.VMEM((2, 3, 2, RB - YR, 128), BF),
            pltpu.VMEM((2, RB - YR, 128), BF),
            pltpu.VMEM((2, RB - YR, 128), BF),
            pltpu.VMEM((256, 128), BF),
            pltpu.VMEM((NDP, 16, 256), BF),
            pltpu.VMEM((NDP, 16, 256), BF),
            dma((7,)),
            dma((NDP,)), dma((NDP,)),
            dma((2, 18)), dma((2, 18)), dma((2, 20)), dma((2, 20)),
            dma((8,)), dma((8,)), dma((2, 4)), dma((2, 4)), dma((2, 3)), dma((2, 3)),
            dma((2, 3)), dma((2, 3)), dma((2,)), dma((2,)),
            dma((NDP,)), dma((NDP,)),
        ],
        compiler_params=pltpu.CompilerParams(
            collective_id=0, has_side_effects=True, vmem_limit_bytes=40 * 1024 * 1024
        ),
        name="comm",
    )(*(pltpu.with_memory_space_constraint(a, pltpu.HBM) for a in operands))

    gt, gg, gate, up, down = pl.pallas_call(
        finish_kernel,
        out_shape=[
            jax.ShapeDtypeStruct((F, TOK), BF),
            jax.ShapeDtypeStruct((2, TOK), F32),
            jax.ShapeDtypeStruct((1, D, HID), BF),
            jax.ShapeDtypeStruct((1, D, HID), BF),
            jax.ShapeDtypeStruct((1, HID, D), BF),
        ],
        in_specs=[vmem] * 5,
        out_specs=[vmem, vmem, hbm, hbm, hbm],
        scratch_shapes=[dma((3,))],
        compiler_params=pltpu.CompilerParams(vmem_limit_bytes=16 * 1024 * 1024),
        name="finish",
    )(*(pltpu.with_memory_space_constraint(a, pltpu.VMEM) for a in results))
    return gt.T, gg.T, gate, up, down


def solution(mesh):
    in_specs = (
        P("dp", "expert"),
        P("dp", "expert"),
        P("dp", None),
        P("dp", None),
        P("dp", None, "expert"),
        P("dp", None, "expert"),
        P("dp", "expert", None),
    )
    out_specs = (
        P("dp", "expert"),
        P("dp", None),
        P("dp", None, "expert"),
        P("dp", None, "expert"),
        P("dp", "expert", None),
    )
    return jax.shard_map(
        per_device, mesh=mesh, in_specs=in_specs, out_specs=out_specs, check_vma=False
    )
```

```python
import functools

import jax
import jax.numpy as jnp
from jax import lax
from jax.experimental import pallas as pl
from jax.experimental.pallas import tpu as pltpu
from jax.sharding import PartitionSpec as P

MESH = pl.DeviceIdType.MESH
BF = jnp.bfloat16
F32 = jnp.float32

CAP = 8
NDP = 16
NEX = 16
F = 448
FA = 256
FB = F - FA
HB = FB // 2
HA = FA // 2
C = 2 * F
D = NEX * F
HID = 128
TOK = 128
SLOTS = NDP * CAP
NEAR = (0, 2, 14, 4, 12, 6, 10, 1)
FAR = (8, 7, 9, 11, 5, 13, 3, 15)
OFFSETS = NEAR + FAR
FH = F // 2
DR = 4 * HID + 16
YR = 144
RB = FH + 16

ORDER = (
    "0own 0Wown 1own 0Aoo", "0Bxl 0Bxr 0Axl 0Axr", "0Boo 1Wown 0Wxl 0Wxr",
    "1Bxl 1Bxr 1Aoo 0Woo", "1Axl 1Axr 1Boo 0Boxl", "1Wxl 1Wxr 1Woo 0Bxo1",
    "0Bxo2 0Aoxl 0Aoxr 0Boxr", "0Axo1 0Axo2 1Bxo1 1Bxo2", "1Boxl 0Woxl 0Woxr 1Boxr",
    "0Wxo 1Aoxl 1Aoxr 0Boxo1", "1Axo1 1Axo2 0Boxo2 1Boxo1", "0Aoxo1 0Aoxo2 1Woxl 1Boxo2",
    "1Woxr 1Wxo 0Woxo 1Aoxo1", "1Aoxo2 0U 1Woxo 1U", "0S 0C0 0C1 0C2",
    "0C3 0C4 0C5 0C6", "0C7 0N0 0N1 0N2", "0N3 0N4 0N5 0N6",
    "0N7 1P2xo 1P2xr 1P2xl", "1Q2 0P2xo 0P2xr 0P2xl", "0Q2 0G02 1B 0B",
    "0G28",
)


def iota(shape, dim):
    return lax.broadcasted_iota(jnp.int32, shape, dim)


def split_gate(row):
    hi = row.astype(BF).astype(F32)
    lo = row - hi
    r = iota((16, row.shape[1]), 0)
    return jnp.where(r == 0, hi, jnp.where(r == 1, lo, 0.0)).astype(BF)


def comm_kernel(
    tok_hbm, cot_hbm, ids_hbm, gates_hbm, wg_hbm, wu_hbm, wd_hbm,
    ret_out, pick_out, gate_out, up_out, down_out,
    ids_ref, gates_ref, wgu, wt, ext, sx, rx, al0, al1, acc, dd, hg,
    dsib, wsib, y_keep, y_send, y_recv, yx_send, yx_recv, x_keep, x_send, x_recv, xy_send, xy_recv,
    rpad, retb, ret,
    w_sem, d_send, d_recv, g_send, g_recv, sib_send, sib_recv,
    ds_send, ds_recv, ws_send, ws_recv, ys_sem, yr_sem, yxs_sem, yxr_sem, xs_sem, xr_sem, xys_sem, xyr_sem,
    b_send, b_recv,
):
    me = lax.axis_index("dp")
    j = lax.axis_index("expert")
    y, x, c = j // 8, (j // 2) % 4, j % 2

    def dev(yy, xx, cc):
        return yy * 8 + xx * 2 + cc

    xr, xl, xo = (x + 1) % 4, (x + 3) % 4, (x + 2) % 4
    yo = 1 - y
    sib, xp, xm, yp = dev(y, x, 1 - c), dev(y, xr, c), dev(y, xl, c), dev(yo, x, c)

    started = []

    barrier = pltpu.get_barrier_semaphore()
    for i in FAR + NEAR[:0:-1]:
        pl.semaphore_signal(barrier, inc=1, device_id=((me + i) % NDP, j), device_id_type=MESH)
    chips = [(y, xr), (y, xl), (y, xo), (yo, x)]
    for yy, xx in chips:
        pl.semaphore_signal(barrier, inc=1, device_id=(me, dev(yy, xx, c)), device_id_type=MESH)
    pl.semaphore_signal(barrier, inc=1, device_id=(me, sib), device_id_type=MESH)

    loads = [
        pltpu.make_async_copy(wg_hbm.at[0], wgu.at[:, 0:HID], w_sem.at[0]),
        pltpu.make_async_copy(wu_hbm.at[0], wgu.at[:, HID : 2 * HID], w_sem.at[1]),
        pltpu.make_async_copy(wd_hbm.at[0], wt.at[2 * HID : 3 * HID, :], w_sem.at[2]),
    ]
    acts = [
        pltpu.make_async_copy(ids_hbm, ids_ref, w_sem.at[5]),
        pltpu.make_async_copy(gates_hbm, gates_ref, w_sem.at[6]),
        pltpu.make_async_copy(tok_hbm, ext.at[0:F, 0:TOK], w_sem.at[3]),
        pltpu.make_async_copy(cot_hbm, ext.at[0:F, TOK : 2 * TOK], w_sem.at[4]),
    ]
    for load in acts + loads:
        load.start()
    acts[0].wait()
    acts[1].wait()

    row = iota((256, TOK), 0)
    ahead = sum(jnp.where(row // 16 == n, o, 0) for n, o in enumerate(OFFSETS))
    expert = (ahead + me) % NDP
    in_first = expert < NDP // 2
    member = jnp.where(in_first, ids_ref[0:1, :], ids_ref[1:2, :]) == expert
    tri = (iota((TOK, TOK), 0) < iota((TOK, TOK), 1)).astype(F32).astype(BF)
    before = jnp.dot(member.astype(F32).astype(BF), tri, preferred_element_type=F32)
    pick = jnp.where(
        jnp.logical_and(member, before == (row % 8).astype(F32)), 1.0, 0.0
    )
    is_x = (row % 16) < 8
    pick_x = jnp.where(is_x, pick, 0.0)
    pick_d = jnp.where(is_x, 0.0, pick)
    pick_out[0] = jnp.where(in_first, pick_x, 0.0).astype(BF)
    pick_out[1] = jnp.where(in_first, 0.0, pick_x).astype(BF)
    pick_out[2] = pick_d.astype(BF)
    gates = gates_ref[...].astype(F32)
    line = iota((512 - F, TOK), 0)
    ext[F:512, 0:TOK] = jnp.where(
        line == 0, gates[0:1, :], jnp.where(line == 1, gates[1:2, :], 0.0)
    ).astype(BF)
    ext[F:512, TOK : 2 * TOK] = jnp.zeros((512 - F, TOK), BF)
    for load in acts[2:]:
        load.wait()
    slots = lax.dot_general(
        jnp.concatenate([pick_x, pick_d], axis=1).astype(BF), ext[...],
        (((1,), (1,)), ((), ())), preferred_element_type=F32,
    ).astype(BF)
    sx[...] = slots.reshape(NDP, 16, 512)
    rx[0] = sx[0]

    r = iota((128, 128), 0)
    k = iota((128, 128), 1)
    perm = jnp.where(k == ((r % 16) // 8) * 64 + (r // 16) * 8 + r % 8, 1.0, 0.0).astype(BF)
    nt = (((1,), (1,)), ((), ()))
    acc[...] = jnp.zeros_like(acc)

    pl.semaphore_wait(barrier, NDP - 1 + len(chips) + 1)

    d_copies = [None]
    for n, o in enumerate(OFFSETS):
        if o:
            copy = pltpu.make_async_remote_copy(
                src_ref=sx.at[n], dst_ref=rx.at[n],
                send_sem=d_send.at[n], recv_sem=d_recv.at[n],
                device_id=((me + o) % NDP, j), device_id_type=MESH,
            )
            copy.start()
            d_copies.append(copy)
            started.append(copy)

    for load in loads:
        load.wait()

    w_copies = []
    for q in range(8):
        copy = pltpu.make_async_remote_copy(
            src_ref=wgu.at[pl.ds(pl.multiple_of(q * C + (1 - c) * F, 16), F)], dst_ref=wsib.at[q],
            send_sem=ws_send.at[q], recv_sem=ws_recv.at[q],
            device_id=(me, sib), device_id_type=MESH,
        )
        copy.start()
        w_copies.append(copy)
        started.append(copy)

    def turn(i, carry):
        at = pl.ds(pl.multiple_of(i * C, 128), C)
        wt[0 : 2 * HID, at] = wgu[at, :].T
        return carry

    lax.fori_loop(0, D // C, turn, 0)

    al = (al0, al1)

    def piece(h, b, lo, n):
        return al[h].at[pl.ds(pl.multiple_of(b * F + lo, 16), n)]

    def move(h, b, lo, n, to, s, sems):
        ref = piece(h, b, lo, n)
        return pltpu.make_async_remote_copy(
            src_ref=ref, dst_ref=ref,
            send_sem=sems[0].at[h, s], recv_sem=sems[1].at[h, s],
            device_id=(me, to), device_id_type=MESH,
        )

    def push(h, b, lo, n, to, s):
        copy = move(h, b, lo, n, to, s, (g_send, g_recv))
        copy.start()
        started.append(copy)

    def share(h, b, lo, n, s):
        copy = move(h, b, lo, n, sib, s, (sib_send, sib_recv))
        copy.start()
        started.append(copy)

    def got(h, b, lo, n, s):
        move(h, b, lo, n, sib, s, (g_send, g_recv)).wait_recv()

    def shared(h, b, lo, n, s):
        move(h, b, lo, n, sib, s, (sib_send, sib_recv)).wait_recv()

    def forward(h, chip):
        at = pl.ds(pl.multiple_of(chip * C, 128), C)
        acc[h] += jnp.dot(wt[:, at], al[h][at, :], preferred_element_type=F32)

    gate_rows = [None, None]

    def own(h):
        for n in range(8 * h, 8 * h + 8):
            if d_copies[n] is not None:
                d_copies[n].wait_recv()
        turned = lax.dot_general(
            rx[8 * h : 8 * h + 8].reshape(128, 512), perm,
            (((0,), (0,)), ((), ())), preferred_element_type=F32,
        )
        al[h][pl.ds(pl.multiple_of(j * F, 16), F), :] = turned[0:F].astype(BF)
        gate_rows[h] = jnp.where(me < NDP // 2, turned[F : F + 1], turned[F + 1 : F + 2])
        push(h, j, FA, FB, xp, 4)
        push(h, j, FA, FB, xm, 5)
        push(h, j, 0, FA, yp, 0)
        push(h, j, 0, FA, xp, 1)
        push(h, j, 0, FA, xm, 2)
        push(h, j, FA, FB, yp, 3)
        share(h, j, 0, FA, 0)
        share(h, j, FA, FB, 1)

    arrivals = {
        "Aoo": ((yo, x), 0, FA, 0, 2, ((0, FA, xp, 6), (0, FA, xm, 7))),
        "Axl": ((y, xl), 0, FA, 1, 5, ((0, HA, xp, 12),)),
        "Axr": ((y, xr), 0, FA, 2, 6, ((HA, HA, xm, 13),)),
        "Boo": ((yo, x), FA, FB, 3, 11, ()),
        "Bxl": ((y, xl), FA, FB, 4, 3, ((FA, HB, xp, 8), (FA, FB, yp, 9))),
        "Bxr": ((y, xr), FA, FB, 5, 4, ((FA + HB, HB, xm, 10), (FA, FB, yp, 11))),
        "Aoxl": ((yo, xl), 0, FA, 6, 9, ((0, HA, xp, 16),)),
        "Aoxr": ((yo, xr), 0, FA, 7, 10, ((HA, HA, xm, 17),)),
        "Bxo1": ((y, xo), FA, HB, 8, 7, ((FA, HB, yp, 14),)),
        "Bxo2": ((y, xo), FA + HB, HB, 10, 8, ((FA + HB, HB, yp, 15),)),
        "Boxl": ((yo, xl), FA, FB, 9, 12, ()),
        "Boxr": ((yo, xr), FA, FB, 11, 13, ()),
        "Axo1": ((y, xo), 0, HA, 12, 14, ()),
        "Axo2": ((y, xo), HA, HA, 13, 15, ()),
        "Boxo1": ((yo, xo), FA, HB, 14, 18, ()),
        "Boxo2": ((yo, xo), FA + HB, HB, 15, 19, ()),
        "Aoxo1": ((yo, xo), 0, HA, 16, 16, ()),
        "Aoxo2": ((yo, xo), HA, HA, 17, 17, ()),
    }
    works = {
        "Wown": ((y, x), ((0, FA, 0), (FA, FB, 1))),
        "Wxl": ((y, xl), ((FA, FB, 3), (0, FA, 5))),
        "Wxr": ((y, xr), ((FA, FB, 4), (0, FA, 6))),
        "Woo": ((yo, x), ((0, FA, 2), (FA, FB, 11))),
        "Woxl": ((yo, xl), ((0, FA, 9), (FA, FB, 12))),
        "Woxr": ((yo, xr), ((0, FA, 10), (FA, FB, 13))),
        "Wxo": ((y, xo), ((FA, HB, 7), (FA + HB, HB, 8), (0, HA, 14), (HA, HA, 15))),
        "Woxo": ((yo, xo), ((0, HA, 16), (HA, HA, 17), (FA, HB, 18), (FA + HB, HB, 19))),
    }

    def arrive(h, name):
        (yy, xx), lo, n, s, to_sib, onward = arrivals[name]
        b = dev(yy, xx, c)
        got(h, b, lo, n, s)
        for first, count, to, sem in onward:
            push(h, b, first, count, to, sem)
        share(h, b, lo, n, to_sib)

    def work(h, name):
        (yy, xx), parts = works[name]
        for lo, n, s in parts:
            shared(h, dev(yy, xx, 1 - c), lo, n, s)
        forward(h, yy * 4 + xx)

    d_sent = [None, None]

    def units(h):
        pg, pu = acc[h, 0:HID, :], acc[h, HID : 2 * HID, :]
        sig = jax.nn.sigmoid(pg)
        act = pg * sig
        hidden = act * pu
        bk = pltpu.roll(acc[h, 2 * HID : 3 * HID, :], 64, 1)
        ok = iota((HID, 128), 1) < 64
        dhid = gate_rows[h] * bk
        dg = jnp.where(ok, dhid * pu * sig * (1.0 + pg * (1.0 - sig)), 0.0)
        du = jnp.where(ok, dhid * act, 0.0)
        lanes = slice(128 * h, 128 * h + 128)
        dd[0:HID, lanes] = dg.astype(BF)
        dd[HID : 2 * HID, lanes] = du.astype(BF)
        dd[2 * HID : 3 * HID, lanes] = pltpu.roll(dg, 64, 1).astype(BF)
        dd[3 * HID : 4 * HID, lanes] = pltpu.roll(du, 64, 1).astype(BF)
        dd[4 * HID : DR, lanes] = split_gate(
            jnp.sum(
                jnp.where(ok, bk * hidden.astype(BF).astype(F32), 0.0), axis=0, keepdims=True
            )
        )
        copy = pltpu.make_async_remote_copy(
            src_ref=dd.at[:, lanes], dst_ref=dsib.at[:, lanes],
            send_sem=ds_send.at[h], recv_sem=ds_recv.at[h],
            device_id=(me, sib), device_id_type=MESH,
        )
        copy.start()
        d_sent[h] = copy
        started.append(copy)
        hg[h] = pltpu.roll(jnp.where(ok, hidden * gate_rows[h], 0.0), 64, 1).astype(BF)

    def term(w, first, d):
        lo = w[pl.ds(first, FH), :]
        hi = w[pl.ds(first + FH, FH), :]
        return jnp.dot(lo, d[0 : 2 * HID, :], preferred_element_type=F32) + jnp.dot(
            hi, d[2 * HID : 4 * HID, :], preferred_element_type=F32
        )

    def gate_total(*blocks):
        total = sum(block.astype(F32) for block in blocks)
        return jnp.sum(total, axis=0, keepdims=True)

    columns = (xo, xr, xl, x)
    y_copies, yx_copies, x_copies, xy_copies = {}, {}, {}, {}

    def send(copies, key, src, dst, send_sem, recv_sem, to):
        copy = pltpu.make_async_remote_copy(
            src_ref=src, dst_ref=dst, send_sem=send_sem, recv_sem=recv_sem,
            device_id=(me, to), device_id_type=MESH,
        )
        copy.start()
        copies[key] = copy
        started.append(copy)

    gate_parts = []

    def with_sibling():
        for copy in w_copies + d_sent:
            copy.wait_recv()
        for h in (0, 1):
            lanes = slice(128 * h, 128 * h + 128)
            gate_parts.append(gate_total(dd[4 * HID : DR, lanes], dsib[4 * HID : DR, lanes]))

    def to_chips(n):
        col, mine = n // 2, n % 2
        chip = (yo, y)[mine] * 4 + columns[col]
        both = term(wgu, pl.multiple_of(chip * C + c * F, 16), dd)
        both = both + term(wsib.at[chip], 0, dsib)
        for h in (1, 0):
            lanes = slice(128 * h, 128 * h + 128)
            part = both[:, lanes]
            gate_part = gate_parts[h]
            if mine:
                y_keep[h, col] = part[0:YR]
            else:
                y_send[h, col] = part[0:YR].astype(BF)
            if col == 3:
                x_keep[h, mine, 0 : FH - YR, :] = part[YR:FH]
                x_keep[h, mine, FH - YR :, :] = jnp.where(
                    iota((16, 128), 0) == 0, gate_part, 0.0
                )
            else:
                x_send[h, col, mine, 0 : FH - YR, :] = part[YR:FH].astype(BF)
                x_send[h, col, mine, FH - YR :, :] = split_gate(gate_part)
            if h == 1:
                leave(h, n)

    def leave(h, n):
        col, mine = n // 2, n % 2
        if not mine:
            send(
                y_copies, (h, col), y_send.at[h, col], y_recv.at[h, col],
                ys_sem.at[h, col], yr_sem.at[h, col], yp,
            )
        elif col < 3:
            send(
                x_copies, (h, col), x_send.at[h, col], x_recv.at[h, col],
                xs_sem.at[h, col], xr_sem.at[h, col], dev(y, columns[col], c),
            )

    def then_x(h, col):
        y_copies[h, col].wait_recv()
        yx_send[h, col] = (y_keep[h, col] + y_recv[h, col].astype(F32)).astype(BF)
        send(
            yx_copies, (h, col), yx_send.at[h, col], yx_recv.at[h, col],
            yxs_sem.at[h, col], yxr_sem.at[h, col], dev(y, columns[col], c),
        )

    def x_total(h, mine):
        total = x_keep[h, mine]
        for col in range(3):
            total = total + x_recv[h, col, mine].astype(F32)
        return total

    def then_y(h):
        for col in range(3):
            x_copies[h, col].wait_recv()
        total = x_total(h, 0)
        xy_send[h, 0 : FH - YR, :] = total[0 : FH - YR].astype(BF)
        xy_send[h, FH - YR :, :] = split_gate(gate_total(total[FH - YR :]))
        send(xy_copies, h, xy_send.at[h], xy_recv.at[h], xys_sem.at[h], xyr_sem.at[h], yp)

    b_copies = []

    def give_back(h):
        second = x_total(h, 1)
        y_copies[h, 3].wait_recv()
        first = y_keep[h, 3] + y_recv[h, 3].astype(F32)
        for col in range(3):
            yx_copies[h, col].wait_recv()
            first = first + yx_recv[h, col].astype(F32)
        xy_copies[h].wait_recv()
        second = second + xy_recv[h].astype(F32)
        rpad[0:YR, :] = first.astype(BF)
        rpad[YR:FH, :] = second[0 : FH - YR].astype(BF)
        rpad[FH:RB, :] = split_gate(gate_total(second[FH - YR :]))
        rpad[RB:256, :] = jnp.zeros((256 - RB, 128), BF)
        rows = lax.dot_general(perm, rpad[...], nt, preferred_element_type=F32)
        retb[8 * h : 8 * h + 8] = rows.astype(BF).reshape(8, 16, 256)
        for n in range(8 * h, 8 * h + 8):
            o = OFFSETS[n]
            if o:
                copy = pltpu.make_async_remote_copy(
                    src_ref=retb.at[n], dst_ref=ret.at[n],
                    send_sem=b_send.at[n], recv_sem=b_recv.at[n],
                    device_id=((me + NDP - o) % NDP, j), device_id_type=MESH,
                )
                copy.start()
                b_copies.append(copy)
                started.append(copy)
            else:
                ret[0] = retb[0]

    def grads(i, carry):
        at = pl.ds(pl.multiple_of(i * C, 128), C)
        near, far = al0[at, :], al1[at, :]
        both = lax.dot_general(near, dd[0 : 2 * HID, 0:128], nt, preferred_element_type=F32)
        both += lax.dot_general(far, dd[0 : 2 * HID, 128:256], nt, preferred_element_type=F32)
        gate_out[at, :] = both[:, 0:HID].astype(BF)
        up_out[at, :] = both[:, HID : 2 * HID].astype(BF)
        down = lax.dot_general(hg[0], near, nt, preferred_element_type=F32)
        down += lax.dot_general(hg[1], far, nt, preferred_element_type=F32)
        down_out[:, at] = down.astype(BF)
        return carry

    for name in " ".join(ORDER).split():
        h, name = int(name[0]), name[1:]
        if name == "own":
            own(h)
        elif name in arrivals:
            arrive(h, name)
        elif name in works:
            work(h, name)
        elif name == "U":
            units(h)
        elif name == "S":
            with_sibling()
        elif name[0] == "C":
            to_chips(int(name[1:]))
        elif name[0] == "N":
            leave(h, int(name[1:]))
        elif name == "Q2":
            then_y(h)
        elif name[:2] == "P2":
            then_x(h, ("xo", "xr", "xl").index(name[2:]))
        elif name == "B":
            give_back(h)
        elif name[0] == "G":
            lax.fori_loop(int(name[1]), int(name[2]), grads, 0)

    for copy in b_copies:
        copy.wait_recv()
    ret_out[...] = ret[...].reshape(256, 256)
    for copy in started:
        copy.wait_send()


def finish_kernel(ret, pick, gate, up, down, gt_out, gg_out, gate_out, up_out, down_out, sems):
    copies = []
    for n in range(4):
        rows, units = pl.ds(n * (D // 4), D // 4), pl.ds(n * (HID // 4), HID // 4)
        copies += [
            pltpu.make_async_copy(gate.at[rows], gate_out.at[0, rows], sems.at[3 * n]),
            pltpu.make_async_copy(up.at[rows], up_out.at[0, rows], sems.at[3 * n + 1]),
            pltpu.make_async_copy(down.at[units], down_out.at[0, units], sems.at[3 * n + 2]),
        ]
    for copy in copies:
        copy.start()
    tn = (((0,), (0,)), ((), ()))
    rows = ret[...]
    one, two, low = (
        lax.dot_general(rows, pick[n], tn, preferred_element_type=F32) for n in range(3)
    )
    gt_out[0:FH, :] = (one + two)[0:FH].astype(BF)
    gt_out[FH:F, :] = low[0:FH].astype(BF)
    gg_out[0:1, :] = one[FH : FH + 1] + one[FH + 1 : FH + 2]
    gg_out[1:2, :] = two[FH : FH + 1] + two[FH + 1 : FH + 2]
    for copy in copies:
        copy.wait()


def per_device(tokens, cotangent, gates, expert_ids, w_gate, w_up, w_down):
    vmem = pl.BlockSpec(memory_space=pltpu.VMEM)
    hbm = pl.BlockSpec(memory_space=pltpu.HBM)
    dma = pltpu.SemaphoreType.DMA
    operands = (tokens.T, cotangent.T, expert_ids.T, gates.T, w_gate, w_up, w_down)
    results = pl.pallas_call(
        comm_kernel,
        out_shape=[
            pltpu.VMEM((256, 256), BF),
            pltpu.VMEM((3, 256, TOK), BF),
            pltpu.VMEM((D, HID), BF),
            pltpu.VMEM((D, HID), BF),
            pltpu.VMEM((HID, D), BF),
        ],
        in_specs=[hbm] * 7,
        out_specs=[vmem] * 5,
        scratch_shapes=[
            pltpu.VMEM((2, TOK), jnp.int32),
            pltpu.VMEM((2, TOK), BF),
            pltpu.VMEM((D, 2 * HID), BF),
            pltpu.VMEM((3 * HID, D), BF),
            pltpu.VMEM((512, 2 * TOK), BF),
            pltpu.VMEM((NDP, 16, 512), BF),
            pltpu.VMEM((NDP, 16, 512), BF),
            pltpu.VMEM((D, 128), BF),
            pltpu.VMEM((D, 128), BF),
            pltpu.VMEM((2, 3 * HID, 128), F32),
            pltpu.VMEM((DR, 256), BF),
            pltpu.VMEM((2, HID, 128), BF),
            pltpu.VMEM((DR, 256), BF),
            pltpu.VMEM((8, F, 2 * HID), BF),
            pltpu.VMEM((2, 4, YR, 128), F32),
            pltpu.VMEM((2, 4, YR, 128), BF),
            pltpu.VMEM((2, 4, YR, 128), BF),
            pltpu.VMEM((2, 3, YR, 128), BF),
            pltpu.VMEM((2, 3, YR, 128), BF),
            pltpu.VMEM((2, 2, RB - YR, 128), F32),
            pltpu.VMEM((2, 3, 2, RB - YR, 128), BF),
            pltpu.VMEM((2, 3, 2, RB - YR, 128), BF),
            pltpu.VMEM((2, RB - YR, 128), BF),
            pltpu.VMEM((2, RB - YR, 128), BF),
            pltpu.VMEM((256, 128), BF),
            pltpu.VMEM((NDP, 16, 256), BF),
            pltpu.VMEM((NDP, 16, 256), BF),
            dma((7,)),
            dma((NDP,)), dma((NDP,)),
            dma((2, 18)), dma((2, 18)), dma((2, 20)), dma((2, 20)),
            dma((2,)), dma((2,)), dma((8,)), dma((8,)), dma((2, 4)), dma((2, 4)), dma((2, 3)), dma((2, 3)),
            dma((2, 3)), dma((2, 3)), dma((2,)), dma((2,)),
            dma((NDP,)), dma((NDP,)),
        ],
        compiler_params=pltpu.CompilerParams(
            collective_id=0, has_side_effects=True, vmem_limit_bytes=40 * 1024 * 1024
        ),
        name="comm",
    )(*(pltpu.with_memory_space_constraint(a, pltpu.HBM) for a in operands))

    gt, gg, gate, up, down = pl.pallas_call(
        finish_kernel,
        out_shape=[
            jax.ShapeDtypeStruct((F, TOK), BF),
            jax.ShapeDtypeStruct((2, TOK), F32),
            jax.ShapeDtypeStruct((1, D, HID), BF),
            jax.ShapeDtypeStruct((1, D, HID), BF),
            jax.ShapeDtypeStruct((1, HID, D), BF),
        ],
        in_specs=[vmem] * 5,
        out_specs=[vmem, vmem, hbm, hbm, hbm],
        scratch_shapes=[dma((12,))],
        compiler_params=pltpu.CompilerParams(vmem_limit_bytes=16 * 1024 * 1024),
        name="finish",
    )(*(pltpu.with_memory_space_constraint(a, pltpu.VMEM) for a in results))
    return gt.T, gg.T, gate, up, down


def solution(mesh):
    in_specs = (
        P("dp", "expert"),
        P("dp", "expert"),
        P("dp", None),
        P("dp", None),
        P("dp", None, "expert"),
        P("dp", None, "expert"),
        P("dp", "expert", None),
    )
    out_specs = (
        P("dp", "expert"),
        P("dp", None),
        P("dp", None, "expert"),
        P("dp", None, "expert"),
        P("dp", "expert", None),
    )
    return jax.shard_map(
        per_device, mesh=mesh, in_specs=in_specs, out_specs=out_specs, check_vma=False
    )
```

```python
import functools

import jax
import jax.numpy as jnp
from jax import lax
from jax.experimental import pallas as pl
from jax.experimental.pallas import tpu as pltpu
from jax.sharding import PartitionSpec as P

MESH = pl.DeviceIdType.MESH
BF = jnp.bfloat16
F32 = jnp.float32

CAP = 8
NDP = 16
NEX = 16
F = 448
FA = 256
FB = F - FA
HB = FB // 2
HA = FA // 2
C = 2 * F
D = NEX * F
HID = 128
TOK = 128
SLOTS = NDP * CAP
NEAR = (0, 2, 14, 4, 12, 6, 10, 1)
FAR = (8, 7, 9, 11, 5, 13, 3, 15)
OFFSETS = NEAR + FAR
FH = F // 2
DR = 4 * HID + 16
YR = 144
RB = FH + 16

ORDER = (
    "0own 1own 0Aoo 0Bxl", "0Bxr 0Axl 0Axr 0Boo", "1Bxl 1Bxr 1Aoo 1Axl",
    "1Axr 0Wown 1Wown 1Boo", "0Wxl 0Wxr 0Woo 0Boxl", "0Bxo1 0Bxo2 0Aoxl 0Aoxr",
    "0Boxr 0Axo1 0Axo2 1Bxo1", "1Bxo2 1Wxl 1Wxr 1Woo", "1Boxl 1Boxr 1Aoxl 1Aoxr",
    "0Woxl 0Woxr 0Wxo 0Boxo1", "1Axo1 1Axo2 1Woxl 0Boxo2", "1Boxo1 0Aoxo1 0Aoxo2 1Boxo2",
    "1Woxr 1Wxo 1Aoxo1 1Aoxo2", "0Woxo 0U 1Woxo 1U", "0S 0C0 0C1 0C2",
    "0C3 0C4 0C5 0C6", "0C7 0N0 0N1 0N2", "0N3 0N4 0N5 0N6",
    "0N7 1P2xo 1P2xr 1P2xl", "1Q2 0P2xo 0P2xr 0P2xl", "0Q2 0G02 1B 0B",
    "0G28",
)


def iota(shape, dim):
    return lax.broadcasted_iota(jnp.int32, shape, dim)


def split_gate(row):
    hi = row.astype(BF).astype(F32)
    lo = row - hi
    r = iota((16, row.shape[1]), 0)
    return jnp.where(r == 0, hi, jnp.where(r == 1, lo, 0.0)).astype(BF)


def comm_kernel(
    tok_hbm, cot_hbm, ids_hbm, gates_hbm, wg_hbm, wu_hbm, wd_hbm,
    ret_out, pick_out, gate_out, up_out, down_out,
    ids_ref, gates_ref, wgu, wt, ext, sx, rx, al0, al1, acc, dd, hg,
    dsib, wsib, y_keep, y_send, y_recv, yx_send, yx_recv, x_keep, x_send, x_recv, xy_send, xy_recv,
    rpad, retb, ret,
    w_sem, d_send, d_recv, g_send, g_recv, sib_send, sib_recv,
    ds_send, ds_recv, ws_send, ws_recv, ys_sem, yr_sem, yxs_sem, yxr_sem, xs_sem, xr_sem, xys_sem, xyr_sem,
    b_send, b_recv,
):
    me = lax.axis_index("dp")
    j = lax.axis_index("expert")
    y, x, c = j // 8, (j // 2) % 4, j % 2

    def dev(yy, xx, cc):
        return yy * 8 + xx * 2 + cc

    xr, xl, xo = (x + 1) % 4, (x + 3) % 4, (x + 2) % 4
    yo = 1 - y
    sib, xp, xm, yp = dev(y, x, 1 - c), dev(y, xr, c), dev(y, xl, c), dev(yo, x, c)

    started = []

    barrier = pltpu.get_barrier_semaphore()
    for i in FAR + NEAR[:0:-1]:
        pl.semaphore_signal(barrier, inc=1, device_id=((me + i) % NDP, j), device_id_type=MESH)
    chips = [(y, xr), (y, xl), (y, xo), (yo, x)]
    for yy, xx in chips:
        pl.semaphore_signal(barrier, inc=1, device_id=(me, dev(yy, xx, c)), device_id_type=MESH)
    pl.semaphore_signal(barrier, inc=1, device_id=(me, sib), device_id_type=MESH)

    loads = [
        pltpu.make_async_copy(wg_hbm.at[0], wgu.at[:, 0:HID], w_sem.at[0]),
        pltpu.make_async_copy(wu_hbm.at[0], wgu.at[:, HID : 2 * HID], w_sem.at[1]),
        pltpu.make_async_copy(wd_hbm.at[0], wt.at[2 * HID : 3 * HID, :], w_sem.at[2]),
    ]
    acts = [
        pltpu.make_async_copy(ids_hbm, ids_ref, w_sem.at[5]),
        pltpu.make_async_copy(gates_hbm, gates_ref, w_sem.at[6]),
        pltpu.make_async_copy(tok_hbm, ext.at[0:F, 0:TOK], w_sem.at[3]),
        pltpu.make_async_copy(cot_hbm, ext.at[0:F, TOK : 2 * TOK], w_sem.at[4]),
    ]
    for load in acts + loads:
        load.start()
    acts[0].wait()
    acts[1].wait()

    row = iota((256, TOK), 0)
    ahead = sum(jnp.where(row // 16 == n, o, 0) for n, o in enumerate(OFFSETS))
    expert = (ahead + me) % NDP
    in_first = expert < NDP // 2
    member = jnp.where(in_first, ids_ref[0:1, :], ids_ref[1:2, :]) == expert
    tri = (iota((TOK, TOK), 0) < iota((TOK, TOK), 1)).astype(F32).astype(BF)
    before = jnp.dot(member.astype(F32).astype(BF), tri, preferred_element_type=F32)
    pick = jnp.where(
        jnp.logical_and(member, before == (row % 8).astype(F32)), 1.0, 0.0
    )
    is_x = (row % 16) < 8
    pick_x = jnp.where(is_x, pick, 0.0)
    pick_d = jnp.where(is_x, 0.0, pick)
    pick_out[0] = jnp.where(in_first, pick_x, 0.0).astype(BF)
    pick_out[1] = jnp.where(in_first, 0.0, pick_x).astype(BF)
    pick_out[2] = pick_d.astype(BF)
    gates = gates_ref[...].astype(F32)
    line = iota((512 - F, TOK), 0)
    ext[F:512, 0:TOK] = jnp.where(
        line == 0, gates[0:1, :], jnp.where(line == 1, gates[1:2, :], 0.0)
    ).astype(BF)
    ext[F:512, TOK : 2 * TOK] = jnp.zeros((512 - F, TOK), BF)
    for load in acts[2:]:
        load.wait()
    slots = lax.dot_general(
        jnp.concatenate([pick_x, pick_d], axis=1).astype(BF), ext[...],
        (((1,), (1,)), ((), ())), preferred_element_type=F32,
    ).astype(BF)
    sx[...] = slots.reshape(NDP, 16, 512)
    rx[0] = sx[0]

    r = iota((128, 128), 0)
    k = iota((128, 128), 1)
    perm = jnp.where(k == ((r % 16) // 8) * 64 + (r // 16) * 8 + r % 8, 1.0, 0.0).astype(BF)
    nt = (((1,), (1,)), ((), ()))
    acc[...] = jnp.zeros_like(acc)

    pl.semaphore_wait(barrier, NDP - 1 + len(chips) + 1)

    d_copies = [None]
    for n, o in enumerate(OFFSETS):
        if o:
            copy = pltpu.make_async_remote_copy(
                src_ref=sx.at[n], dst_ref=rx.at[n],
                send_sem=d_send.at[n], recv_sem=d_recv.at[n],
                device_id=((me + o) % NDP, j), device_id_type=MESH,
            )
            copy.start()
            d_copies.append(copy)
            started.append(copy)

    for load in loads:
        load.wait()

    w_copies = []
    for q in range(8):
        copy = pltpu.make_async_remote_copy(
            src_ref=wgu.at[pl.ds(pl.multiple_of(q * C + (1 - c) * F, 16), F)], dst_ref=wsib.at[q],
            send_sem=ws_send.at[q], recv_sem=ws_recv.at[q],
            device_id=(me, sib), device_id_type=MESH,
        )
        copy.start()
        w_copies.append(copy)
        started.append(copy)

    def turn(i, carry):
        at = pl.ds(pl.multiple_of(i * C, 128), C)
        wt[0 : 2 * HID, at] = wgu[at, :].T
        return carry

    lax.fori_loop(0, D // C, turn, 0)

    al = (al0, al1)

    def piece(h, b, lo, n):
        return al[h].at[pl.ds(pl.multiple_of(b * F + lo, 16), n)]

    def move(h, b, lo, n, to, s, sems):
        ref = piece(h, b, lo, n)
        return pltpu.make_async_remote_copy(
            src_ref=ref, dst_ref=ref,
            send_sem=sems[0].at[h, s], recv_sem=sems[1].at[h, s],
            device_id=(me, to), device_id_type=MESH,
        )

    def push(h, b, lo, n, to, s):
        copy = move(h, b, lo, n, to, s, (g_send, g_recv))
        copy.start()
        started.append(copy)

    def share(h, b, lo, n, s):
        copy = move(h, b, lo, n, sib, s, (sib_send, sib_recv))
        copy.start()
        started.append(copy)

    def got(h, b, lo, n, s):
        move(h, b, lo, n, sib, s, (g_send, g_recv)).wait_recv()

    def shared(h, b, lo, n, s):
        move(h, b, lo, n, sib, s, (sib_send, sib_recv)).wait_recv()

    def forward(h, chip):
        at = pl.ds(pl.multiple_of(chip * C, 128), C)
        acc[h] += jnp.dot(wt[:, at], al[h][at, :], preferred_element_type=F32)

    gate_rows = [None, None]

    def own(h):
        for n in range(8 * h, 8 * h + 8):
            if d_copies[n] is not None:
                d_copies[n].wait_recv()
        turned = lax.dot_general(
            rx[8 * h : 8 * h + 8].reshape(128, 512), perm,
            (((0,), (0,)), ((), ())), preferred_element_type=F32,
        )
        al[h][pl.ds(pl.multiple_of(j * F, 16), F), :] = turned[0:F].astype(BF)
        gate_rows[h] = jnp.where(me < NDP // 2, turned[F : F + 1], turned[F + 1 : F + 2])
        push(h, j, FA, FB, xp, 4)
        push(h, j, FA, FB, xm, 5)
        push(h, j, 0, FA, yp, 0)
        push(h, j, 0, FA, xp, 1)
        push(h, j, 0, FA, xm, 2)
        push(h, j, FA, FB, yp, 3)
        share(h, j, 0, FA, 0)
        share(h, j, FA, FB, 1)

    arrivals = {
        "Aoo": ((yo, x), 0, FA, 0, 2, ((0, FA, xp, 6), (0, FA, xm, 7))),
        "Axl": ((y, xl), 0, FA, 1, 5, ((0, HA, xp, 12),)),
        "Axr": ((y, xr), 0, FA, 2, 6, ((HA, HA, xm, 13),)),
        "Boo": ((yo, x), FA, FB, 3, 11, ()),
        "Bxl": ((y, xl), FA, FB, 4, 3, ((FA, HB, xp, 8), (FA, FB, yp, 9))),
        "Bxr": ((y, xr), FA, FB, 5, 4, ((FA + HB, HB, xm, 10), (FA, FB, yp, 11))),
        "Aoxl": ((yo, xl), 0, FA, 6, 9, ((0, HA, xp, 16),)),
        "Aoxr": ((yo, xr), 0, FA, 7, 10, ((HA, HA, xm, 17),)),
        "Bxo1": ((y, xo), FA, HB, 8, 7, ((FA, HB, yp, 14),)),
        "Bxo2": ((y, xo), FA + HB, HB, 10, 8, ((FA + HB, HB, yp, 15),)),
        "Boxl": ((yo, xl), FA, FB, 9, 12, ()),
        "Boxr": ((yo, xr), FA, FB, 11, 13, ()),
        "Axo1": ((y, xo), 0, HA, 12, 14, ()),
        "Axo2": ((y, xo), HA, HA, 13, 15, ()),
        "Boxo1": ((yo, xo), FA, HB, 14, 18, ()),
        "Boxo2": ((yo, xo), FA + HB, HB, 15, 19, ()),
        "Aoxo1": ((yo, xo), 0, HA, 16, 16, ()),
        "Aoxo2": ((yo, xo), HA, HA, 17, 17, ()),
    }
    works = {
        "Wown": ((y, x), ((0, FA, 0), (FA, FB, 1))),
        "Wxl": ((y, xl), ((FA, FB, 3), (0, FA, 5))),
        "Wxr": ((y, xr), ((FA, FB, 4), (0, FA, 6))),
        "Woo": ((yo, x), ((0, FA, 2), (FA, FB, 11))),
        "Woxl": ((yo, xl), ((0, FA, 9), (FA, FB, 12))),
        "Woxr": ((yo, xr), ((0, FA, 10), (FA, FB, 13))),
        "Wxo": ((y, xo), ((FA, HB, 7), (FA + HB, HB, 8), (0, HA, 14), (HA, HA, 15))),
        "Woxo": ((yo, xo), ((0, HA, 16), (HA, HA, 17), (FA, HB, 18), (FA + HB, HB, 19))),
    }

    def arrive(h, name):
        (yy, xx), lo, n, s, to_sib, onward = arrivals[name]
        b = dev(yy, xx, c)
        got(h, b, lo, n, s)
        for first, count, to, sem in onward:
            push(h, b, first, count, to, sem)
        share(h, b, lo, n, to_sib)

    def work(h, name):
        (yy, xx), parts = works[name]
        for lo, n, s in parts:
            shared(h, dev(yy, xx, 1 - c), lo, n, s)
        forward(h, yy * 4 + xx)

    d_sent = [None, None]

    def units(h):
        pg, pu = acc[h, 0:HID, :], acc[h, HID : 2 * HID, :]
        sig = jax.nn.sigmoid(pg)
        act = pg * sig
        hidden = act * pu
        bk = pltpu.roll(acc[h, 2 * HID : 3 * HID, :], 64, 1)
        ok = iota((HID, 128), 1) < 64
        dhid = gate_rows[h] * bk
        dg = jnp.where(ok, dhid * pu * sig * (1.0 + pg * (1.0 - sig)), 0.0)
        du = jnp.where(ok, dhid * act, 0.0)
        lanes = slice(128 * h, 128 * h + 128)
        dd[0:HID, lanes] = dg.astype(BF)
        dd[HID : 2 * HID, lanes] = du.astype(BF)
        dd[2 * HID : 3 * HID, lanes] = pltpu.roll(dg, 64, 1).astype(BF)
        dd[3 * HID : 4 * HID, lanes] = pltpu.roll(du, 64, 1).astype(BF)
        dd[4 * HID : DR, lanes] = split_gate(
            jnp.sum(
                jnp.where(ok, bk * hidden.astype(BF).astype(F32), 0.0), axis=0, keepdims=True
            )
        )
        copy = pltpu.make_async_remote_copy(
            src_ref=dd.at[:, lanes], dst_ref=dsib.at[:, lanes],
            send_sem=ds_send.at[h], recv_sem=ds_recv.at[h],
            device_id=(me, sib), device_id_type=MESH,
        )
        copy.start()
        d_sent[h] = copy
        started.append(copy)
        hg[h] = pltpu.roll(jnp.where(ok, hidden * gate_rows[h], 0.0), 64, 1).astype(BF)

    def term(w, first, d):
        lo = w[pl.ds(first, FH), :]
        hi = w[pl.ds(first + FH, FH), :]
        return jnp.dot(lo, d[0 : 2 * HID, :], preferred_element_type=F32) + jnp.dot(
            hi, d[2 * HID : 4 * HID, :], preferred_element_type=F32
        )

    def gate_total(*blocks):
        total = sum(block.astype(F32) for block in blocks)
        return jnp.sum(total, axis=0, keepdims=True)

    columns = (xo, xr, xl, x)
    y_copies, yx_copies, x_copies, xy_copies = {}, {}, {}, {}

    def send(copies, key, src, dst, send_sem, recv_sem, to):
        copy = pltpu.make_async_remote_copy(
            src_ref=src, dst_ref=dst, send_sem=send_sem, recv_sem=recv_sem,
            device_id=(me, to), device_id_type=MESH,
        )
        copy.start()
        copies[key] = copy
        started.append(copy)

    gate_parts = []

    def with_sibling():
        for copy in w_copies + d_sent:
            copy.wait_recv()
        for h in (0, 1):
            lanes = slice(128 * h, 128 * h + 128)
            gate_parts.append(gate_total(dd[4 * HID : DR, lanes], dsib[4 * HID : DR, lanes]))

    def to_chips(n):
        col, mine = n // 2, n % 2
        chip = (yo, y)[mine] * 4 + columns[col]
        both = term(wgu, pl.multiple_of(chip * C + c * F, 16), dd)
        both = both + term(wsib.at[chip], 0, dsib)
        for h in (1, 0):
            lanes = slice(128 * h, 128 * h + 128)
            part = both[:, lanes]
            gate_part = gate_parts[h]
            if mine:
                y_keep[h, col] = part[0:YR]
            else:
                y_send[h, col] = part[0:YR].astype(BF)
            if col == 3:
                x_keep[h, mine, 0 : FH - YR, :] = part[YR:FH]
                x_keep[h, mine, FH - YR :, :] = jnp.where(
                    iota((16, 128), 0) == 0, gate_part, 0.0
                )
            else:
                x_send[h, col, mine, 0 : FH - YR, :] = part[YR:FH].astype(BF)
                x_send[h, col, mine, FH - YR :, :] = split_gate(gate_part)
            if h == 1:
                leave(h, n)

    def leave(h, n):
        col, mine = n // 2, n % 2
        if not mine:
            send(
                y_copies, (h, col), y_send.at[h, col], y_recv.at[h, col],
                ys_sem.at[h, col], yr_sem.at[h, col], yp,
            )
        elif col < 3:
            send(
                x_copies, (h, col), x_send.at[h, col], x_recv.at[h, col],
                xs_sem.at[h, col], xr_sem.at[h, col], dev(y, columns[col], c),
            )

    def then_x(h, col):
        y_copies[h, col].wait_recv()
        yx_send[h, col] = (y_keep[h, col] + y_recv[h, col].astype(F32)).astype(BF)
        send(
            yx_copies, (h, col), yx_send.at[h, col], yx_recv.at[h, col],
            yxs_sem.at[h, col], yxr_sem.at[h, col], dev(y, columns[col], c),
        )

    def x_total(h, mine):
        total = x_keep[h, mine]
        for col in range(3):
            total = total + x_recv[h, col, mine].astype(F32)
        return total

    def then_y(h):
        for col in range(3):
            x_copies[h, col].wait_recv()
        total = x_total(h, 0)
        xy_send[h, 0 : FH - YR, :] = total[0 : FH - YR].astype(BF)
        xy_send[h, FH - YR :, :] = split_gate(gate_total(total[FH - YR :]))
        send(xy_copies, h, xy_send.at[h], xy_recv.at[h], xys_sem.at[h], xyr_sem.at[h], yp)

    b_copies = []

    def give_back(h):
        second = x_total(h, 1)
        y_copies[h, 3].wait_recv()
        first = y_keep[h, 3] + y_recv[h, 3].astype(F32)
        for col in range(3):
            yx_copies[h, col].wait_recv()
            first = first + yx_recv[h, col].astype(F32)
        xy_copies[h].wait_recv()
        second = second + xy_recv[h].astype(F32)
        rpad[0:YR, :] = first.astype(BF)
        rpad[YR:FH, :] = second[0 : FH - YR].astype(BF)
        rpad[FH:RB, :] = split_gate(gate_total(second[FH - YR :]))
        rpad[RB:256, :] = jnp.zeros((256 - RB, 128), BF)
        rows = lax.dot_general(perm, rpad[...], nt, preferred_element_type=F32)
        retb[8 * h : 8 * h + 8] = rows.astype(BF).reshape(8, 16, 256)
        for n in range(8 * h, 8 * h + 8):
            o = OFFSETS[n]
            if o:
                copy = pltpu.make_async_remote_copy(
                    src_ref=retb.at[n], dst_ref=ret.at[n],
                    send_sem=b_send.at[n], recv_sem=b_recv.at[n],
                    device_id=((me + NDP - o) % NDP, j), device_id_type=MESH,
                )
                copy.start()
                b_copies.append(copy)
                started.append(copy)
            else:
                ret[0] = retb[0]

    def grads(i, carry):
        at = pl.ds(pl.multiple_of(i * C, 128), C)
        near, far = al0[at, :], al1[at, :]
        both = lax.dot_general(near, dd[0 : 2 * HID, 0:128], nt, preferred_element_type=F32)
        both += lax.dot_general(far, dd[0 : 2 * HID, 128:256], nt, preferred_element_type=F32)
        gate_out[at, :] = both[:, 0:HID].astype(BF)
        up_out[at, :] = both[:, HID : 2 * HID].astype(BF)
        down = lax.dot_general(hg[0], near, nt, preferred_element_type=F32)
        down += lax.dot_general(hg[1], far, nt, preferred_element_type=F32)
        down_out[:, at] = down.astype(BF)
        return carry

    for name in " ".join(ORDER).split():
        h, name = int(name[0]), name[1:]
        if name == "own":
            own(h)
        elif name in arrivals:
            arrive(h, name)
        elif name in works:
            work(h, name)
        elif name == "U":
            units(h)
        elif name == "S":
            with_sibling()
        elif name[0] == "C":
            to_chips(int(name[1:]))
        elif name[0] == "N":
            leave(h, int(name[1:]))
        elif name == "Q2":
            then_y(h)
        elif name[:2] == "P2":
            then_x(h, ("xo", "xr", "xl").index(name[2:]))
        elif name == "B":
            give_back(h)
        elif name[0] == "G":
            lax.fori_loop(int(name[1]), int(name[2]), grads, 0)

    for copy in b_copies:
        copy.wait_recv()
    ret_out[...] = ret[...].reshape(256, 256)
    for copy in started:
        copy.wait_send()


def finish_kernel(ret, pick, gate, up, down, gt_out, gg_out, gate_out, up_out, down_out, sems):
    copies = []
    for n in range(4):
        rows, units = pl.ds(n * (D // 4), D // 4), pl.ds(n * (HID // 4), HID // 4)
        copies += [
            pltpu.make_async_copy(gate.at[rows], gate_out.at[0, rows], sems.at[3 * n]),
            pltpu.make_async_copy(up.at[rows], up_out.at[0, rows], sems.at[3 * n + 1]),
            pltpu.make_async_copy(down.at[units], down_out.at[0, units], sems.at[3 * n + 2]),
        ]
    for copy in copies:
        copy.start()
    tn = (((0,), (0,)), ((), ()))
    rows = ret[...]
    one, two, low = (
        lax.dot_general(rows, pick[n], tn, preferred_element_type=F32) for n in range(3)
    )
    gt_out[0:FH, :] = (one + two)[0:FH].astype(BF)
    gt_out[FH:F, :] = low[0:FH].astype(BF)
    gg_out[0:1, :] = one[FH : FH + 1] + one[FH + 1 : FH + 2]
    gg_out[1:2, :] = two[FH : FH + 1] + two[FH + 1 : FH + 2]
    for copy in copies:
        copy.wait()


def per_device(tokens, cotangent, gates, expert_ids, w_gate, w_up, w_down):
    vmem = pl.BlockSpec(memory_space=pltpu.VMEM)
    hbm = pl.BlockSpec(memory_space=pltpu.HBM)
    dma = pltpu.SemaphoreType.DMA
    operands = (tokens.T, cotangent.T, expert_ids.T, gates.T, w_gate, w_up, w_down)
    results = pl.pallas_call(
        comm_kernel,
        out_shape=[
            pltpu.VMEM((256, 256), BF),
            pltpu.VMEM((3, 256, TOK), BF),
            pltpu.VMEM((D, HID), BF),
            pltpu.VMEM((D, HID), BF),
            pltpu.VMEM((HID, D), BF),
        ],
        in_specs=[hbm] * 7,
        out_specs=[vmem] * 5,
        scratch_shapes=[
            pltpu.VMEM((2, TOK), jnp.int32),
            pltpu.VMEM((2, TOK), BF),
            pltpu.VMEM((D, 2 * HID), BF),
            pltpu.VMEM((3 * HID, D), BF),
            pltpu.VMEM((512, 2 * TOK), BF),
            pltpu.VMEM((NDP, 16, 512), BF),
            pltpu.VMEM((NDP, 16, 512), BF),
            pltpu.VMEM((D, 128), BF),
            pltpu.VMEM((D, 128), BF),
            pltpu.VMEM((2, 3 * HID, 128), F32),
            pltpu.VMEM((DR, 256), BF),
            pltpu.VMEM((2, HID, 128), BF),
            pltpu.VMEM((DR, 256), BF),
            pltpu.VMEM((8, F, 2 * HID), BF),
            pltpu.VMEM((2, 4, YR, 128), F32),
            pltpu.VMEM((2, 4, YR, 128), BF),
            pltpu.VMEM((2, 4, YR, 128), BF),
            pltpu.VMEM((2, 3, YR, 128), BF),
            pltpu.VMEM((2, 3, YR, 128), BF),
            pltpu.VMEM((2, 2, RB - YR, 128), F32),
            pltpu.VMEM((2, 3, 2, RB - YR, 128), BF),
            pltpu.VMEM((2, 3, 2, RB - YR, 128), BF),
            pltpu.VMEM((2, RB - YR, 128), BF),
            pltpu.VMEM((2, RB - YR, 128), BF),
            pltpu.VMEM((256, 128), BF),
            pltpu.VMEM((NDP, 16, 256), BF),
            pltpu.VMEM((NDP, 16, 256), BF),
            dma((7,)),
            dma((NDP,)), dma((NDP,)),
            dma((2, 18)), dma((2, 18)), dma((2, 20)), dma((2, 20)),
            dma((2,)), dma((2,)), dma((8,)), dma((8,)), dma((2, 4)), dma((2, 4)), dma((2, 3)), dma((2, 3)),
            dma((2, 3)), dma((2, 3)), dma((2,)), dma((2,)),
            dma((NDP,)), dma((NDP,)),
        ],
        compiler_params=pltpu.CompilerParams(
            collective_id=0, has_side_effects=True, vmem_limit_bytes=40 * 1024 * 1024
        ),
        name="comm",
    )(*(pltpu.with_memory_space_constraint(a, pltpu.HBM) for a in operands))

    gt, gg, gate, up, down = pl.pallas_call(
        finish_kernel,
        out_shape=[
            jax.ShapeDtypeStruct((F, TOK), BF),
            jax.ShapeDtypeStruct((2, TOK), F32),
            jax.ShapeDtypeStruct((1, D, HID), BF),
            jax.ShapeDtypeStruct((1, D, HID), BF),
            jax.ShapeDtypeStruct((1, HID, D), BF),
        ],
        in_specs=[vmem] * 5,
        out_specs=[vmem, vmem, hbm, hbm, hbm],
        scratch_shapes=[dma((12,))],
        compiler_params=pltpu.CompilerParams(vmem_limit_bytes=16 * 1024 * 1024),
        name="finish",
    )(*(pltpu.with_memory_space_constraint(a, pltpu.VMEM) for a in results))
    return gt.T, gg.T, gate, up, down


def solution(mesh):
    in_specs = (
        P("dp", "expert"),
        P("dp", "expert"),
        P("dp", None),
        P("dp", None),
        P("dp", None, "expert"),
        P("dp", None, "expert"),
        P("dp", "expert", None),
    )
    out_specs = (
        P("dp", "expert"),
        P("dp", None),
        P("dp", None, "expert"),
        P("dp", None, "expert"),
        P("dp", "expert", None),
    )
    return jax.shard_map(
        per_device, mesh=mesh, in_specs=in_specs, out_specs=out_specs, check_vma=False
    )
```
